32 devices in a mesh: dp: 8 (over z, y), mp: 4 (over x, core).
Axes of the slice: x: 2, y: 2, z: 4, core: 2. Of those that a mesh axis runs over, the one named last changes fastest.
Arguments:
- frames: bfloat16 [2048, 1024], P('dp'), may hold values from -24 to 24
- proj_in: bfloat16 [1024, 2, 1024], P(None, None, 'mp'), may hold values from -0.1875 to 0.1875
- depthwise: float32 [31, 1024], P(None, 'mp'), may hold values from -1 to 1
- bn_gain: float32 [1024], P('mp'), may hold values from 0.5 to 1.5
- bn_shift: float32 [1024], P('mp'), may hold values from -3 to 3
- proj_out: bfloat16 [1024, 1024], P(None, 'mp'), may hold values from -0.1875 to 0.1875
- grad_out: bfloat16 [2048, 1024], P('dp'), may hold values from -6 to 6
- counts: int32 [8], replicated, may hold values from 1 to 2, as said below
- lengths: int32 [8, 2], P('dp'), may hold values from 1 to 255, as said below
Outputs:
- frame_grad: bfloat16 [2048, 1024], P('dp', 'mp')
- in_grad: float32 [1024, 2, 1024], P('dp', None, 'mp')
- out_grad: float32 [1024, 1024], P('dp', 'mp')
- depth_grad: float32 [31, 1024], P(None, 'mp')
- gain_grad: float32 [1024], P('mp')
- shift_grad: float32 [1024], P('mp')
The draws below stay inside these ranges and needn't reach their ends.
Inputs may be any that keep to these rules, and one draw needn't show every extreme that they name: `counts`: some device holds 2 live blocks. lengths[d] sums to 128 * counts[d]; on some device with 2 live blocks one utterance holds all frames but one for each other utterance.
All inputs are finite; a program needn't handle non-finite values.
Results may differ from the reference program's by a relative error of at most 0.0095.
Values may be sent and summed in bfloat16 or wider, within the bound.
A program may use at most 64 MiB of HBM per device.

```python
import jax
import jax.numpy as jnp
from jax import lax

D = 1024
K = 31
BLOCK = 128
BLK_DEV = 2
UTT_DEV = 2
FRAMES = 2048
N_DP = 8
N_MP = 4


def block_plan(key):
    base_key = jax.random.fold_in(key, 7)
    count_key, pick_key, split_key = jax.random.split(base_key, 3)
    counts = jax.random.randint(count_key, (N_DP,), 1, BLK_DEV + 1, dtype=jnp.int32)
    chosen = jax.random.randint(pick_key, (), 0, N_DP, dtype=jnp.int32)
    is_chosen = jnp.arange(N_DP, dtype=jnp.int32) == chosen
    counts = jnp.where(is_chosen, BLK_DEV, counts).astype(jnp.int32)
    weights = jax.random.randint(split_key, (N_DP, UTT_DEV), 1, 1001, dtype=jnp.int32)
    spare_frames = counts * BLOCK - UTT_DEV
    shares = 1 + spare_frames[:, None] * weights // jnp.sum(weights, axis=1, keepdims=True)
    leading = shares[:, :-1]
    final_len = counts * BLOCK - jnp.sum(leading, axis=1)
    lengths = jnp.concatenate([leading, final_len[:, None]], axis=1).astype(jnp.int32)
    utt_pos = jnp.arange(UTT_DEV, dtype=jnp.int32)
    extreme = jnp.where(utt_pos == UTT_DEV - 1, BLK_DEV * BLOCK - UTT_DEV + 1, 1).astype(jnp.int32)
    lengths = jnp.where(is_chosen[:, None], extreme[None, :], lengths).astype(jnp.int32)
    return (counts, lengths)


def draw_counts(key, part):
    return block_plan(key)[0]


def draw_lengths(key, part):
    return block_plan(key)[1]


def draw_frames(key, part):
    base_key = jax.random.fold_in(key, 11)
    noise_key, scale_key, pick_key, pair_key = jax.random.split(base_key, 4)
    rows_dev = BLK_DEV * BLOCK
    dev_of_row = (jnp.arange(FRAMES, dtype=jnp.int32) // rows_dev).astype(jnp.int32)
    ramp = jnp.arange(N_DP, dtype=jnp.float32) / float(max(N_DP - 1, 1))
    chosen = jax.random.randint(pick_key, (), 0, N_DP, dtype=jnp.int32)
    is_chosen = jnp.arange(N_DP, dtype=jnp.int32) == chosen
    pairing = jax.random.permutation(pair_key, N_DP).astype(jnp.int32)
    col_block = (jnp.arange(D, dtype=jnp.int32) // (D // N_DP)).astype(jnp.int32)
    spike = jnp.where(col_block[None, :] == pairing[dev_of_row][:, None], 3.0, 1.0).astype(jnp.float32)
    base_vals = jax.random.normal(noise_key, (FRAMES, D), jnp.float32)
    jitter = jnp.exp(jax.random.uniform(scale_key, (N_DP,), jnp.float32, 0.0, 1.1939225))
    dev_scale = (1.0 + 2.0 * ramp) * jitter
    dev_scale = jnp.where(is_chosen, 12.0, dev_scale)
    values = base_vals * dev_scale[dev_of_row][:, None] * spike
    return jnp.clip(values, -24.0, 24.0).astype(jnp.bfloat16)


def spiked(array, own_key, source, target, shards_of, factor):
    owner, partner = [(jnp.arange(array.shape[dim]) // (array.shape[dim] // shards_of)).reshape([-1 if axis == dim else 1 for axis in range(array.ndim)]) for dim in (source, target)]
    chosen = jax.random.permutation(own_key, shards_of)[partner]
    strong = (owner == chosen) | (owner == (partner + shards_of // 2) % shards_of)
    return jnp.where(strong, factor * array, array)


def steps_of(stream_key, dims, cuts, low, high):
    factor_of, own = 1.0, jax.random.fold_in(stream_key, 6)
    for dim, parts in cuts:
        steps = jnp.exp(jax.random.uniform(jax.random.fold_in(own, dim), (parts,), jnp.float32, low / len(cuts), high / len(cuts)))
        factor_of = factor_of * jnp.repeat(steps, dims[dim] // parts).reshape([-1 if axis == dim else 1 for axis in range(len(dims))])
    return factor_of


def bell_draw(rng, extent, spread, most, pieces=(), held_as=jnp.bfloat16):
    array = spread * jax.random.normal(rng, extent, jnp.float32)
    if pieces:
        array = array * steps_of(rng, extent, pieces, -0.22, 0.18)
    return jnp.clip(array, -most, most).astype(held_as)


def bell_draw_with(own_key, dims, deviation, limit, shards, heavy, kind=jnp.bfloat16):
    array = deviation * jax.random.normal(own_key, dims, jnp.float32)
    if shards:
        array = array * steps_of(own_key, dims, shards, -0.22, 0.18)
    return jnp.clip(spiked(array, jax.random.fold_in(own_key, 3), *heavy), -limit, limit).astype(kind)


def setup_inputs(seed: int = 0) -> dict:
    splits = jax.random.split(jax.random.key(seed), 10)
    return {
        "frames": draw_frames(jax.random.fold_in(splits[9], 71), 0),
        "proj_in": bell_draw(splits[1], (D, 2, D), D ** -0.5, 0.1875, ((2, 4),)),
        "depthwise": bell_draw(splits[2], (K, D), K ** -0.5, 1.0, ((1, 4),), jnp.float32),
        "bn_gain": jnp.clip(0.5 + 1.0 * jax.random.uniform(splits[3], (D,), jnp.float32) ** steps_of(splits[3], (D,), ((0, 4),), -0.2, 0.2), 0.5, 1.5),
        "bn_shift": bell_draw(splits[4], (D,), 0.5, 3.0, ((0, 4),), jnp.float32),
        "proj_out": bell_draw(splits[5], (D, D), D ** -0.5, 0.1875, ((1, 4),)),
        "grad_out": bell_draw_with(splits[6], (FRAMES, D), 1.0, 6.0, ((0, 8),), (0, 1, 8, 2.0)),
        "counts": draw_counts(jax.random.fold_in(splits[9], 71), 0),
        "lengths": draw_lengths(jax.random.fold_in(splits[9], 71), 0),
    }


def time_shift(values, offset, fill_value):
    if offset > 0:
        pad_part = jnp.full((offset,) + values.shape[1:], fill_value, values.dtype)
        return jnp.concatenate([values[offset:], pad_part], axis=0)
    if offset < 0:
        pad_part = jnp.full((-offset,) + values.shape[1:], fill_value, values.dtype)
        return jnp.concatenate([pad_part, values[:offset]], axis=0)
    return values

def layout(counts, lengths):
    slots_dev = BLK_DEV * BLOCK
    position = jnp.arange(slots_dev, dtype=jnp.int32)
    utt_ends = jnp.cumsum(lengths, axis=1).astype(jnp.int32)
    seg_index = lax.optimization_barrier(jnp.sum((position[None, :, None] >= utt_ends[:, None, :]).astype(jnp.int32), axis=2)).astype(jnp.int32)
    live_mask = (position[None, :] < (counts * BLOCK).astype(jnp.int32)[:, None]).astype(jnp.float32)
    owner_id = (jnp.arange(N_DP, dtype=jnp.int32)[:, None] * (UTT_DEV + 1) + seg_index).astype(jnp.int32)
    return (owner_id.reshape(-1), live_mask.reshape(-1)[:, None])

def reference(frames, proj_in, depthwise, bn_gain, bn_shift, proj_out, grad_out, counts, lengths):
    owner_id, live_col = layout(counts, lengths)
    frame_total = (jnp.sum(counts) * BLOCK).astype(jnp.float32)
    radius = K // 2
    pre_act = jnp.dot(frames, proj_in.reshape(D, 2 * D), preferred_element_type=jnp.float32).reshape(-1, 2, D)
    value_half = pre_act[:, 0]
    gate_sig = jax.nn.sigmoid(pre_act[:, 1])
    glu_out = (value_half * gate_sig * live_col).astype(jnp.bfloat16)
    glu_float = lax.optimization_barrier(glu_out).astype(jnp.float32)
    conv_out = jnp.zeros(glu_float.shape, jnp.float32)
    for tap_index in range(K):
        offset = tap_index - radius
        same_utt = (time_shift(owner_id, offset, -1) == owner_id).astype(jnp.float32)[:, None] * live_col
        conv_out = conv_out + depthwise[tap_index] * (time_shift(glu_float, offset, 0.0) * same_utt)
    mean_val = lax.optimization_barrier(jnp.sum(conv_out, axis=0)) / frame_total
    square_mean = lax.optimization_barrier(jnp.sum(conv_out * conv_out, axis=0)) / frame_total
    inv_std = lax.rsqrt(square_mean - mean_val * mean_val + 1e-05)
    normed = (conv_out - mean_val) * inv_std
    scaled = normed * bn_gain + bn_shift
    sig_scaled = jax.nn.sigmoid(scaled)
    hidden = (scaled * sig_scaled * live_col).astype(jnp.bfloat16)
    grad_hidden = jnp.dot(grad_out, proj_out, preferred_element_type=jnp.float32) * live_col
    grad_scaled = grad_hidden * sig_scaled * (1.0 + scaled * (1.0 - sig_scaled))
    shift_grad = lax.optimization_barrier(jnp.sum(grad_scaled, axis=0))
    gain_grad = lax.optimization_barrier(jnp.sum(grad_scaled * normed, axis=0))
    grad_conv = live_col * bn_gain * inv_std * (grad_scaled - shift_grad / frame_total - normed * gain_grad / frame_total)
    depth_rows = []
    grad_glu = jnp.zeros(glu_float.shape, jnp.float32)
    for tap_index in range(K):
        offset = tap_index - radius
        same_utt = (time_shift(owner_id, offset, -1) == owner_id).astype(jnp.float32)[:, None] * live_col
        depth_rows.append(lax.optimization_barrier(jnp.sum(grad_conv * (time_shift(glu_float, offset, 0.0) * same_utt), axis=0)))
        back_same = (time_shift(owner_id, -offset, -1) == owner_id).astype(jnp.float32)[:, None] * live_col
        grad_glu = grad_glu + depthwise[tap_index] * time_shift(grad_conv, -offset, 0.0) * back_same
    depth_grad = jnp.stack(depth_rows)
    grad_value = grad_glu * gate_sig
    grad_gate = grad_glu * value_half * gate_sig * (1.0 - gate_sig)
    grad_pre = jnp.stack([grad_value, grad_gate], axis=1).astype(jnp.bfloat16)
    group_width = D // N_MP
    grad_groups = grad_pre.reshape(-1, 2, N_MP, group_width)
    proj_groups = proj_in.reshape(D, 2, N_MP, group_width)
    frame_sum = jnp.zeros((grad_pre.shape[0], D), jnp.float32)
    for group_index in range(N_MP):
        left_part = grad_groups[:, :, group_index].reshape(-1, 2 * group_width)
        right_part = proj_groups[:, :, group_index].reshape(D, 2 * group_width)
        partial_value = lax.dot_general(left_part, right_part, (((1,), (1,)), ((), ())), preferred_element_type=jnp.float32)
        frame_sum = frame_sum + lax.optimization_barrier(partial_value.astype(jnp.bfloat16)).astype(jnp.float32)
    frame_grad = frame_sum.astype(jnp.bfloat16)
    in_grad = lax.dot_general(frames, grad_pre.reshape(-1, 2 * D), (((0,), (0,)), ((), ())), preferred_element_type=jnp.float32).reshape(D, 2, D)
    out_grad = lax.dot_general(grad_out, hidden, (((0,), (0,)), ((), ())), preferred_element_type=jnp.float32)
    return (frame_grad, in_grad, out_grad, depth_grad, gain_grad, shift_grad)
```

```python
import functools

import jax
import jax.numpy as jnp
from jax import lax
from jax.experimental import pallas as pl
from jax.experimental.pallas import tpu as pltpu
from jax.sharding import PartitionSpec as P

BLOCK = 128


def time_shift(values, offset, fill_value):
    if offset > 0:
        pad_part = jnp.full((offset,) + values.shape[1:], fill_value, values.dtype)
        return jnp.concatenate([values[offset:], pad_part], axis=0)
    if offset < 0:
        pad_part = jnp.full((-offset,) + values.shape[1:], fill_value, values.dtype)
        return jnp.concatenate([pad_part, values[:offset]], axis=0)
    return values


def tap_term(glu_float, owner_id, live_col, offset):
    same_utt = (time_shift(owner_id, offset, -1) == owner_id).astype(jnp.float32)[
        :, None
    ] * live_col
    return time_shift(glu_float, offset, 0.0) * same_utt


def shards(frames, proj_in, depthwise, bn_gain, bn_shift, proj_out, grad_out, counts, lengths):
    frames_dev = frames.shape[0]
    model_width = frames.shape[1]
    channels = proj_in.shape[2]
    tap_count = depthwise.shape[0]
    radius = tap_count // 2
    rows_dev = model_width // lax.axis_size("dp")
    position = jnp.arange(frames_dev, dtype=jnp.int32)
    utt_ends = jnp.cumsum(lengths[0])
    owner_id = jnp.sum((position[:, None] >= utt_ends[None, :]).astype(jnp.int32), axis=1)
    my_count = counts[lax.axis_index("dp")]
    live_col = (position < my_count * BLOCK).astype(jnp.float32)[:, None]
    frame_total = (jnp.sum(counts) * BLOCK).astype(jnp.float32)
    proj_flat = proj_in.reshape(model_width, 2 * channels)
    pre_act = jnp.dot(frames, proj_flat, preferred_element_type=jnp.float32)
    value_half = pre_act[:, :channels]
    gate_sig = jax.nn.sigmoid(pre_act[:, channels:])
    glu_out = (value_half * gate_sig * live_col).astype(jnp.bfloat16)
    glu_float = lax.optimization_barrier(glu_out).astype(jnp.float32)
    conv_out = jnp.zeros((frames_dev, channels), jnp.float32)
    for tap_index in range(tap_count):
        conv_out = conv_out + depthwise[tap_index] * tap_term(
            glu_float, owner_id, live_col, tap_index - radius
        )
    sum_val, sum_sq = lax.psum(
        (jnp.sum(conv_out, axis=0), jnp.sum(conv_out * conv_out, axis=0)), "dp"
    )
    mean_val = sum_val / frame_total
    square_mean = sum_sq / frame_total
    inv_std = lax.rsqrt(square_mean - mean_val * mean_val + 1e-05)
    normed = (conv_out - mean_val) * inv_std
    scaled = normed * bn_gain + bn_shift
    sig_scaled = jax.nn.sigmoid(scaled)
    hidden = (scaled * sig_scaled * live_col).astype(jnp.bfloat16)
    grad_hidden = jnp.dot(grad_out, proj_out, preferred_element_type=jnp.float32) * live_col
    grad_scaled = grad_hidden * sig_scaled * (1.0 + scaled * (1.0 - sig_scaled))
    local_shift = jnp.sum(grad_scaled, axis=0)
    local_gain = jnp.sum(grad_scaled * normed, axis=0)
    shift_grad, gain_grad = lax.psum((local_shift, local_gain), "dp")
    grad_conv = (
        live_col
        * bn_gain
        * inv_std
        * (grad_scaled - shift_grad / frame_total - normed * gain_grad / frame_total)
    )
    depth_rows = []
    for tap_index in range(tap_count):
        depth_rows.append(
            jnp.sum(grad_conv * tap_term(glu_float, owner_id, live_col, tap_index - radius), axis=0)
        )
    depth_grad = lax.psum(jnp.stack(depth_rows), "dp")
    grad_glu = jnp.zeros((frames_dev, channels), jnp.float32)
    for tap_index in range(tap_count):
        offset = tap_index - radius
        back_same = (time_shift(owner_id, -offset, -1) == owner_id).astype(jnp.float32)[
            :, None
        ] * live_col
        grad_glu = grad_glu + depthwise[tap_index] * time_shift(grad_conv, -offset, 0.0) * back_same
    grad_value = grad_glu * gate_sig
    grad_gate = grad_glu * value_half * gate_sig * (1.0 - gate_sig)
    grad_flat = jnp.concatenate([grad_value, grad_gate], axis=1).astype(jnp.bfloat16)
    frame_term = lax.dot_general(
        grad_flat, proj_flat, (((1,), (1,)), ((), ())), preferred_element_type=jnp.float32
    )
    frame_grad = lax.psum_scatter(
        frame_term.astype(jnp.bfloat16), "mp", scatter_dimension=1, tiled=True
    )
    summed = lax.psum_scatter(
        jnp.concatenate(
            [
                lax.dot_general(
                    frames, grad_flat, (((0,), (0,)), ((), ())), preferred_element_type=jnp.float32
                ),
                lax.dot_general(
                    grad_out, hidden, (((0,), (0,)), ((), ())), preferred_element_type=jnp.float32
                ),
            ],
            axis=1,
        ),
        "dp",
        scatter_dimension=0,
        tiled=True,
    )
    in_flat = summed[:, : 2 * channels]
    out_grad = summed[:, 2 * channels :]
    in_grad = in_flat.reshape(rows_dev, 2, channels)
    return (frame_grad, in_grad, out_grad, depth_grad, gain_grad, shift_grad)


GAP = 16
NT = (((1,), (1,)), ((), ()))
TN = (((0,), (0,)), ((), ()))


def dot(a, b, dims=(((1,), (0,)), ((), ()))):
    return lax.dot_general(a, b, dims, preferred_element_type=jnp.float32)


def remote(src, dst, send_sem, recv_sem, dp, mp):
    return pltpu.make_async_remote_copy(
        src_ref=src,
        dst_ref=dst,
        send_sem=send_sem,
        recv_sem=recv_sem,
        device_id=(dp, mp),
        device_id_type=pl.DeviceIdType.MESH,
    )


def fused(
    n_dp, n_mp,
    frames, proj, taps, gain, shift, proj_out, grad_out, counts, lengths,
    o_frame, o_in, o_out, o_depth, o_gain, o_shift,
    place, live, fg, gg, gpad, cpad, val, gate, conv, gh, gs, gp,
    st1, st1_s, st1_r, st2, st2_s, st2_r,
    oy_s, oy_r, okeep, oz_s, oz_r, oys_sem, oyr_sem, ozs_sem, ozr_sem,
    iy_s, iy_r, ikeep, iz_s, iz_r, iys_sem, iyr_sem, izs_sem, izr_sem,
    f_s, f_r, fs_sem, fr_sem,
    d_s, d_r, ds_sem, dr_sem, e_r, es_sem, er_sem,
):
    rows, chans = conv.shape
    slots = frames.shape[0]
    tap_count = taps.shape[0]
    radius = tap_count // 2
    me = lax.axis_index("dp")
    mp = lax.axis_index("mp")
    nz = n_dp // 2
    my_y = lax.rem(me, 2)
    my_z = me // 2
    piece = o_in.shape[0]
    group = o_frame.shape[1]

    barrier = pltpu.get_barrier_semaphore()
    for k in range(1, n_dp):
        pl.semaphore_signal(
            barrier, inc=1, device_id=(lax.rem(me + k, n_dp), mp),
            device_id_type=pl.DeviceIdType.MESH,
        )
    for k in range(1, n_mp):
        pl.semaphore_signal(
            barrier, inc=1, device_id=(me, lax.rem(mp + k, n_mp)),
            device_id_type=pl.DeviceIdType.MESH,
        )

    def exchange(buf, s_sem, r_sem):
        for k in range(1, n_dp):
            remote(buf.at[me], buf.at[me], s_sem.at[k - 1], r_sem.at[k - 1],
                   lax.rem(me + k, n_dp), mp).start()

    def exchange_wait(buf, s_sem, r_sem):
        for k in range(1, n_dp):
            who = lax.rem(me + n_dp - k, n_dp)
            c = remote(buf.at[who], buf.at[who], s_sem.at[k - 1], r_sem.at[k - 1], who, mp)
            c.wait_recv()

    def exchange_sent(buf, s_sem, r_sem):
        for k in range(1, n_dp):
            remote(buf.at[me], buf.at[me], s_sem.at[k - 1], r_sem.at[k - 1],
                   lax.rem(me + k, n_dp), mp).wait_send()

    def total_of(buf):
        acc = buf[0]
        for p in range(1, n_dp):
            acc = acc + buf[p]
        return acc

    order = list(range(1, nz)) + [0]

    def y_copy(k, s, r, s_sem, r_sem):
        return remote(s.at[k], r.at[k], s_sem.at[k], r_sem.at[k], my_z * 2 + 1 - my_y, mp)

    def z_copy(k, s, r, s_sem, r_sem):
        return remote(s.at[k], r.at[k], s_sem.at[k], r_sem.at[k],
                      lax.rem(my_z + k, nz) * 2 + my_y, mp)

    def scatter_start(left, right, y_s, y_r, keep, ys_sem, yr_sem):
        for k in order:
            other = lax.rem(my_z + k, nz) * 2 + 1 - my_y
            cols = pl.ds(pl.multiple_of(other * piece, piece), piece)
            y_s[k] = dot(left[:, cols], right, TN).astype(jnp.bfloat16)
            y_copy(k, y_s, y_r, ys_sem, yr_sem).start()
        for k in order:
            mine = lax.rem(my_z + k, nz) * 2 + my_y
            cols = pl.ds(pl.multiple_of(mine * piece, piece), piece)
            keep[k] = dot(left[:, cols], right, TN)

    def scatter_mid(y_s, y_r, keep, z_s, z_r, ys_sem, yr_sem, zs_sem, zr_sem):
        for k in order:
            y_copy(k, y_s, y_r, ys_sem, yr_sem).wait_recv()
            if k:
                z_s[k] = (keep[k] + y_r[k].astype(jnp.float32)).astype(jnp.bfloat16)
                z_copy(k, z_s, z_r, zs_sem, zr_sem).start()

    def scatter_end(out, y_s, y_r, keep, z_s, z_r, ys_sem, yr_sem, zs_sem, zr_sem):
        acc = keep[0] + y_r[0].astype(jnp.float32)
        for k in range(1, nz):
            z_copy(k, z_s, z_r, zs_sem, zr_sem).wait_recv()
            acc = acc + z_r[k].astype(jnp.float32)
        out[...] = acc
        for k in range(nz):
            y_copy(k, y_s, y_r, ys_sem, yr_sem).wait_send()
            if k:
                z_copy(k, z_s, z_r, zs_sem, zr_sem).wait_send()

    my_live = counts[me] * BLOCK
    total = counts[0]
    for p in range(1, n_dp):
        total = total + counts[p]
    frame_total = (total * BLOCK).astype(jnp.float32)
    r_id = lax.broadcasted_iota(jnp.int32, (rows, slots), 0)
    s_id = lax.broadcasted_iota(jnp.int32, (rows, slots), 1)
    target = s_id
    end = 0
    for u in range(lengths.shape[1] - 1):
        end = end + lengths[0, u]
        target = target + jnp.where(s_id >= end, GAP, 0)
    place[...] = jnp.where((r_id == target) & (s_id < my_live), 1.0, 0.0).astype(jnp.bfloat16)
    put = place[...]
    live[...] = dot(put, jnp.ones((slots, chans), jnp.bfloat16))
    fg[...] = dot(put, frames[...]).astype(jnp.bfloat16)
    pre = dot(fg[...], proj[...])
    v = pre[:, :chans]
    g = jax.nn.sigmoid(pre[:, chans:])
    val[...] = v
    gate[...] = g
    pad = jnp.zeros((GAP, chans), jnp.float32)
    gpad[:GAP] = pad
    gpad[GAP + rows:] = pad
    cpad[:GAP] = pad
    cpad[GAP + rows:] = pad
    gpad[GAP:GAP + rows] = (v * g * live[...]).astype(jnp.bfloat16).astype(jnp.float32)

    half = rows // 2
    chunks = [(a, c) for a in range(0, rows, half) for c in range(0, chans, 128)]
    for a, c in chunks:
        acc = jnp.zeros((half, 128), jnp.float32)
        for k in range(tap_count):
            first = GAP + a + k - radius
            acc = acc + taps[k:k + 1, c:c + 128] * gpad[first:first + half, c:c + 128]
        conv[a:a + half, c:c + 128] = acc * live[a:a + half, c:c + 128]
    cv = conv[...]
    zero6 = jnp.zeros((6, chans), jnp.float32)
    st1[me] = jnp.concatenate(
        [jnp.sum(cv, axis=0, keepdims=True), jnp.sum(cv * cv, axis=0, keepdims=True), zero6], axis=0
    )
    pl.semaphore_wait(barrier, n_dp + n_mp - 2)
    exchange(st1, st1_s, st1_r)

    gg[...] = dot(put, grad_out[...]).astype(jnp.bfloat16)
    gh[...] = dot(gg[...], proj_out[...])

    exchange_wait(st1, st1_s, st1_r)
    sums = total_of(st1)
    mean = sums[0:1] / frame_total
    inv = lax.rsqrt(sums[1:2] / frame_total - mean * mean + 1e-05)
    normed = (conv[...] - mean) * inv
    scaled = normed * gain[...] + shift[...]
    sig = jax.nn.sigmoid(scaled)
    hidden = (scaled * sig * live[...]).astype(jnp.bfloat16)
    gscaled = gh[...] * live[...] * sig * (1.0 + scaled * (1.0 - sig))
    gs[...] = gscaled
    conv[...] = normed
    st2[me] = jnp.concatenate(
        [
            jnp.sum(gscaled, axis=0, keepdims=True),
            jnp.sum(gscaled * normed, axis=0, keepdims=True),
            zero6,
        ],
        axis=0,
    )
    exchange(st2, st2_s, st2_r)
    scatter_start(gg, hidden, oy_s, oy_r, okeep, oys_sem, oyr_sem)

    exchange_wait(st2, st2_s, st2_r)
    sums = total_of(st2)
    o_shift[...] = sums[0:1]
    o_gain[...] = sums[1:2]
    cpad[GAP:GAP + rows] = (
        live[...] * (gain[...] * inv)
        * (gs[...] - sums[0:1] / frame_total - conv[...] * (sums[1:2] / frame_total))
    )
    for a, c in chunks:
        acc = jnp.zeros((half, 128), jnp.float32)
        for k in range(tap_count):
            first = GAP + a + radius - k
            acc = acc + taps[k:k + 1, c:c + 128] * cpad[first:first + half, c:c + 128]
        acc = acc * live[a:a + half, c:c + 128]
        gt = gate[a:a + half, c:c + 128]
        gval = acc * gt
        gp[a:a + half, c:c + 128] = gval.astype(jnp.bfloat16)
        ggate = gval * val[a:a + half, c:c + 128] * (1.0 - gt)
        gp[a:a + half, chans + c:chans + c + 128] = ggate.astype(jnp.bfloat16)

    scatter_start(fg, gp[...], iy_s, iy_r, ikeep, iys_sem, iyr_sem)
    scatter_mid(oy_s, oy_r, okeep, oz_s, oz_r, oys_sem, oyr_sem, ozs_sem, ozr_sem)

    def f_copy(k):
        return remote(f_s.at[k], f_r.at[k], fs_sem.at[k], fr_sem.at[k],
                      me, lax.rem(mp + k, n_mp))

    back = dot(place[...], gp[...], TN).astype(jnp.bfloat16)
    for k in list(range(1, n_mp)) + [0]:
        peer = lax.rem(mp + k, n_mp)
        part = proj[pl.ds(pl.multiple_of(peer * group, group), group), :]
        f_s[k] = dot(back, part, NT).astype(jnp.bfloat16)
        if k:
            f_copy(k).start()

    scatter_mid(iy_s, iy_r, ikeep, iz_s, iz_r, iys_sem, iyr_sem, izs_sem, izr_sem)

    per = -(-tap_count // n_dp)
    d_s[...] = jnp.zeros(d_s.shape, jnp.float32)
    for c in range(0, chans, 128):
        grad_c = cpad[GAP:GAP + rows, c:c + 128]
        for k in range(tap_count):
            first = GAP + k - radius
            d_s[k // per, k % per:k % per + 1, c:c + 128] = jnp.sum(
                grad_c * gpad[first:first + rows, c:c + 128], axis=0, keepdims=True
            )

    def d_copy(k):
        peer = lax.rem(me + k, n_dp)
        return remote(d_s.at[peer], d_r.at[k], ds_sem.at[k], dr_sem.at[k], peer, mp)

    for k in range(1, n_dp):
        d_copy(k).start()
    acc = d_s[me]
    for k in range(1, n_dp):
        d_copy(k).wait_recv()
        acc = acc + d_r[k]
    e_r[me] = acc
    exchange(e_r, es_sem, er_sem)

    scatter_end(o_out, oy_s, oy_r, okeep, oz_s, oz_r, oys_sem, oyr_sem, ozs_sem, ozr_sem)
    facc = f_s[0].astype(jnp.float32)
    for k in range(1, n_mp):
        f_copy(k).wait_recv()
        facc = facc + f_r[k].astype(jnp.float32)
    o_frame[...] = facc.astype(jnp.bfloat16)
    exchange_wait(e_r, es_sem, er_sem)
    for p in range(n_dp):
        many = min(per, tap_count - p * per)
        if many > 0:
            o_depth[p * per:p * per + many] = e_r[p, :many]
    scatter_end(o_in, iy_s, iy_r, ikeep, iz_s, iz_r, iys_sem, iyr_sem, izs_sem, izr_sem)
    exchange_sent(st1, st1_s, st1_r)
    exchange_sent(st2, st2_s, st2_r)
    exchange_sent(e_r, es_sem, er_sem)
    for k in range(1, n_mp):
        f_copy(k).wait_send()
    for k in range(1, n_dp):
        d_copy(k).wait_send()


def fused_shards(
    frames, proj_in, depthwise, bn_gain, bn_shift, proj_out, grad_out, counts, lengths
):
    n_dp, n_mp = lax.axis_size("dp"), lax.axis_size("mp")
    slots, width = frames.shape
    chans = proj_in.shape[2]
    tap_count = depthwise.shape[0]
    rows = slots + GAP * (lengths.shape[1] - 1)
    piece = width // n_dp
    group = width // n_mp
    nz = n_dp // 2
    per8 = -(-(-(-tap_count // n_dp)) // 8) * 8
    f32, bf16 = jnp.float32, jnp.bfloat16
    vm, dma = pltpu.VMEM, pltpu.SemaphoreType.DMA
    sem_pair = [dma((n_dp,)), dma((n_dp,))]

    def ring(wide):
        shape = (nz, piece, wide)
        return [vm(shape, bf16), vm(shape, bf16), vm(shape, f32), vm(shape, bf16),
                vm(shape, bf16)] + [dma((nz,))] * 4

    full = vm((rows, chans), f32)
    padded = vm((rows + 2 * GAP, chans), f32)
    in_vmem = pl.BlockSpec(memory_space=pltpu.VMEM)
    in_smem = pl.BlockSpec(memory_space=pltpu.SMEM)
    frame_grad, in_flat, out_grad, depth_grad, gain_grad, shift_grad = pl.pallas_call(
        functools.partial(fused, n_dp, n_mp),
        out_shape=[
            jax.ShapeDtypeStruct((slots, group), bf16),
            jax.ShapeDtypeStruct((piece, 2 * chans), f32),
            jax.ShapeDtypeStruct((piece, chans), f32),
            jax.ShapeDtypeStruct((tap_count, chans), f32),
            jax.ShapeDtypeStruct((1, chans), f32),
            jax.ShapeDtypeStruct((1, chans), f32),
        ],
        in_specs=[in_vmem] * 7 + [in_smem] * 2,
        out_specs=[in_vmem] * 6,
        scratch_shapes=[
            vm((rows, slots), bf16), full, vm((rows, width), bf16), vm((rows, width), bf16),
            padded, padded, full, full, full, full, full, vm((rows, 2 * chans), bf16),
            vm((n_dp, 8, chans), f32), *sem_pair, vm((n_dp, 8, chans), f32), *sem_pair,
            *ring(chans), *ring(2 * chans),
            vm((n_mp, slots, group), bf16), vm((n_mp, slots, group), bf16),
            dma((n_mp,)), dma((n_mp,)),
            vm((n_dp, per8, chans), f32), vm((n_dp, per8, chans), f32), *sem_pair,
            vm((n_dp, per8, chans), f32), *sem_pair,
        ],
        compiler_params=pltpu.CompilerParams(
            collective_id=0, has_side_effects=True, vmem_limit_bytes=48 * 1024 * 1024
        ),
    )(
        frames, proj_in.reshape(width, 2 * chans), depthwise, bn_gain[None], bn_shift[None],
        proj_out, grad_out, counts, lengths,
    )
    return (
        frame_grad, in_flat.reshape(piece, 2, chans), out_grad, depth_grad,
        gain_grad.reshape(chans), shift_grad.reshape(chans),
    )


def pick(*args):
    n_dp = lax.axis_size("dp")
    frames, proj_in, taps = args[0], args[1], args[2]
    fits = (
        n_dp % 2 == 0 and n_dp <= 16 and frames.shape[1] % (128 * n_dp) == 0
        and proj_in.shape[2] % 128 == 0 and frames.shape[0] % 16 == 0
        and taps.shape[0] // 2 <= GAP
    )
    return (fused_shards if fits else shards)(*args)


def solution(mesh):
    placed = (
        P("dp", None),
        P(None, None, "mp"),
        P(None, "mp"),
        P("mp"),
        P("mp"),
        P(None, "mp"),
        P("dp", None),
        P(),
        P("dp", None),
    )
    return jax.shard_map(
        pick,
        mesh=mesh,
        in_specs=placed,
        out_specs=(
            P("dp", "mp"),
            P("dp", None, "mp"),
            P("dp", "mp"),
            P(None, "mp"),
            P("mp"),
            P("mp"),
        ),
        check_vma=False,
    )
```

```python
import functools

import jax
import jax.numpy as jnp
from jax import lax
from jax.experimental import pallas as pl
from jax.experimental.pallas import tpu as pltpu
from jax.sharding import PartitionSpec as P

BLOCK = 128


def time_shift(values, offset, fill_value):
    if offset > 0:
        pad_part = jnp.full((offset,) + values.shape[1:], fill_value, values.dtype)
        return jnp.concatenate([values[offset:], pad_part], axis=0)
    if offset < 0:
        pad_part = jnp.full((-offset,) + values.shape[1:], fill_value, values.dtype)
        return jnp.concatenate([pad_part, values[:offset]], axis=0)
    return values


def tap_term(glu_float, owner_id, live_col, offset):
    same_utt = (time_shift(owner_id, offset, -1) == owner_id).astype(jnp.float32)[
        :, None
    ] * live_col
    return time_shift(glu_float, offset, 0.0) * same_utt


def shards(frames, proj_in, depthwise, bn_gain, bn_shift, proj_out, grad_out, counts, lengths):
    frames_dev = frames.shape[0]
    model_width = frames.shape[1]
    channels = proj_in.shape[2]
    tap_count = depthwise.shape[0]
    radius = tap_count // 2
    rows_dev = model_width // lax.axis_size("dp")
    position = jnp.arange(frames_dev, dtype=jnp.int32)
    utt_ends = jnp.cumsum(lengths[0])
    owner_id = jnp.sum((position[:, None] >= utt_ends[None, :]).astype(jnp.int32), axis=1)
    my_count = counts[lax.axis_index("dp")]
    live_col = (position < my_count * BLOCK).astype(jnp.float32)[:, None]
    frame_total = (jnp.sum(counts) * BLOCK).astype(jnp.float32)
    proj_flat = proj_in.reshape(model_width, 2 * channels)
    pre_act = jnp.dot(frames, proj_flat, preferred_element_type=jnp.float32)
    value_half = pre_act[:, :channels]
    gate_sig = jax.nn.sigmoid(pre_act[:, channels:])
    glu_out = (value_half * gate_sig * live_col).astype(jnp.bfloat16)
    glu_float = lax.optimization_barrier(glu_out).astype(jnp.float32)
    conv_out = jnp.zeros((frames_dev, channels), jnp.float32)
    for tap_index in range(tap_count):
        conv_out = conv_out + depthwise[tap_index] * tap_term(
            glu_float, owner_id, live_col, tap_index - radius
        )
    sum_val, sum_sq = lax.psum(
        (jnp.sum(conv_out, axis=0), jnp.sum(conv_out * conv_out, axis=0)), "dp"
    )
    mean_val = sum_val / frame_total
    square_mean = sum_sq / frame_total
    inv_std = lax.rsqrt(square_mean - mean_val * mean_val + 1e-05)
    normed = (conv_out - mean_val) * inv_std
    scaled = normed * bn_gain + bn_shift
    sig_scaled = jax.nn.sigmoid(scaled)
    hidden = (scaled * sig_scaled * live_col).astype(jnp.bfloat16)
    grad_hidden = jnp.dot(grad_out, proj_out, preferred_element_type=jnp.float32) * live_col
    grad_scaled = grad_hidden * sig_scaled * (1.0 + scaled * (1.0 - sig_scaled))
    local_shift = jnp.sum(grad_scaled, axis=0)
    local_gain = jnp.sum(grad_scaled * normed, axis=0)
    shift_grad, gain_grad = lax.psum((local_shift, local_gain), "dp")
    grad_conv = (
        live_col
        * bn_gain
        * inv_std
        * (grad_scaled - shift_grad / frame_total - normed * gain_grad / frame_total)
    )
    depth_rows = []
    for tap_index in range(tap_count):
        depth_rows.append(
            jnp.sum(grad_conv * tap_term(glu_float, owner_id, live_col, tap_index - radius), axis=0)
        )
    depth_grad = lax.psum(jnp.stack(depth_rows), "dp")
    grad_glu = jnp.zeros((frames_dev, channels), jnp.float32)
    for tap_index in range(tap_count):
        offset = tap_index - radius
        back_same = (time_shift(owner_id, -offset, -1) == owner_id).astype(jnp.float32)[
            :, None
        ] * live_col
        grad_glu = grad_glu + depthwise[tap_index] * time_shift(grad_conv, -offset, 0.0) * back_same
    grad_value = grad_glu * gate_sig
    grad_gate = grad_glu * value_half * gate_sig * (1.0 - gate_sig)
    grad_flat = jnp.concatenate([grad_value, grad_gate], axis=1).astype(jnp.bfloat16)
    frame_term = lax.dot_general(
        grad_flat, proj_flat, (((1,), (1,)), ((), ())), preferred_element_type=jnp.float32
    )
    frame_grad = lax.psum_scatter(
        frame_term.astype(jnp.bfloat16), "mp", scatter_dimension=1, tiled=True
    )
    summed = lax.psum_scatter(
        jnp.concatenate(
            [
                lax.dot_general(
                    frames, grad_flat, (((0,), (0,)), ((), ())), preferred_element_type=jnp.float32
                ),
                lax.dot_general(
                    grad_out, hidden, (((0,), (0,)), ((), ())), preferred_element_type=jnp.float32
                ),
            ],
            axis=1,
        ),
        "dp",
        scatter_dimension=0,
        tiled=True,
    )
    in_flat = summed[:, : 2 * channels]
    out_grad = summed[:, 2 * channels :]
    in_grad = in_flat.reshape(rows_dev, 2, channels)
    return (frame_grad, in_grad, out_grad, depth_grad, gain_grad, shift_grad)


GAP = 16
NT = (((1,), (1,)), ((), ()))
TN = (((0,), (0,)), ((), ()))


def dot(a, b, dims=(((1,), (0,)), ((), ()))):
    return lax.dot_general(a, b, dims, preferred_element_type=jnp.float32)


def remote(src, dst, send_sem, recv_sem, dp, mp):
    return pltpu.make_async_remote_copy(
        src_ref=src,
        dst_ref=dst,
        send_sem=send_sem,
        recv_sem=recv_sem,
        device_id=(dp, mp),
        device_id_type=pl.DeviceIdType.MESH,
    )


def fused(
    n_dp, n_mp,
    frames, proj, taps, gain, shift, proj_out, grad_out, counts, lengths,
    o_frame, o_in, o_out, o_depth, o_gain, o_shift,
    place, live, fg, gg, gpad, cpad, val, gate, conv, gh, gs, gp,
    st1, st1_s, st1_r, st2, st2_s, st2_r,
    f_s, f_r, fs_sem, fr_sem,
    d_s, d_r, ds_sem, dr_sem, e_r, es_sem, er_sem,
    *ring_refs,
):
    out_ring = ring_refs[:9]
    in_rings = [ring_refs[i:i + 9] for i in range(9, len(ring_refs), 9)]
    rows, chans = conv.shape
    slots = frames.shape[0]
    tap_count = taps.shape[0]
    radius = tap_count // 2
    me = lax.axis_index("dp")
    mp = lax.axis_index("mp")
    nz = n_dp // 2
    my_y = lax.rem(me, 2)
    my_z = me // 2
    piece = o_in.shape[0]
    group = o_frame.shape[1]

    barrier = pltpu.get_barrier_semaphore()
    for k in range(1, n_dp):
        pl.semaphore_signal(
            barrier, inc=1, device_id=(lax.rem(me + k, n_dp), mp),
            device_id_type=pl.DeviceIdType.MESH,
        )
    for k in range(1, n_mp):
        pl.semaphore_signal(
            barrier, inc=1, device_id=(me, lax.rem(mp + k, n_mp)),
            device_id_type=pl.DeviceIdType.MESH,
        )

    def exchange(buf, s_sem, r_sem):
        for k in range(1, n_dp):
            remote(buf.at[me], buf.at[me], s_sem.at[k - 1], r_sem.at[k - 1],
                   lax.rem(me + k, n_dp), mp).start()

    def exchange_wait(buf, s_sem, r_sem):
        for k in range(1, n_dp):
            who = lax.rem(me + n_dp - k, n_dp)
            c = remote(buf.at[who], buf.at[who], s_sem.at[k - 1], r_sem.at[k - 1], who, mp)
            c.wait_recv()

    def exchange_sent(buf, s_sem, r_sem):
        for k in range(1, n_dp):
            remote(buf.at[me], buf.at[me], s_sem.at[k - 1], r_sem.at[k - 1],
                   lax.rem(me + k, n_dp), mp).wait_send()

    def total_of(buf):
        acc = buf[0]
        for p in range(1, n_dp):
            acc = acc + buf[p]
        return acc

    order = list(range(1, nz)) + [0]

    def y_copy(k, s, r, s_sem, r_sem):
        return remote(s.at[k], r.at[k], s_sem.at[k], r_sem.at[k], my_z * 2 + 1 - my_y, mp)

    def z_copy(k, s, r, s_sem, r_sem):
        return remote(s.at[k], r.at[k], s_sem.at[k], r_sem.at[k],
                      lax.rem(my_z + k, nz) * 2 + my_y, mp)

    def scatter_send(ring, left, right):
        y_s, y_r, _, _, _, ys_sem, yr_sem, _, _ = ring
        for k in order:
            other = lax.rem(my_z + k, nz) * 2 + 1 - my_y
            cols = pl.ds(pl.multiple_of(other * piece, piece), piece)
            y_s[k] = dot(left[:, cols], right, TN).astype(jnp.bfloat16)
            y_copy(k, y_s, y_r, ys_sem, yr_sem).start()

    def scatter_keep(ring, left, right):
        for k in order:
            mine = lax.rem(my_z + k, nz) * 2 + my_y
            cols = pl.ds(pl.multiple_of(mine * piece, piece), piece)
            ring[2][k] = dot(left[:, cols], right, TN)

    def scatter_mid(ring, k):
        y_s, y_r, keep, z_s, z_r, ys_sem, yr_sem, zs_sem, zr_sem = ring
        y_copy(k, y_s, y_r, ys_sem, yr_sem).wait_recv()
        if k:
            z_s[k] = (keep[k] + y_r[k].astype(jnp.float32)).astype(jnp.bfloat16)
            z_copy(k, z_s, z_r, zs_sem, zr_sem).start()

    def scatter_end(ring):
        y_s, y_r, keep, z_s, z_r, ys_sem, yr_sem, zs_sem, zr_sem = ring
        acc = keep[0] + y_r[0].astype(jnp.float32)
        for k in range(1, nz):
            z_copy(k, z_s, z_r, zs_sem, zr_sem).wait_recv()
            acc = acc + z_r[k].astype(jnp.float32)
        return acc

    def scatter_sent(ring):
        y_s, y_r, keep, z_s, z_r, ys_sem, yr_sem, zs_sem, zr_sem = ring
        for k in range(nz):
            y_copy(k, y_s, y_r, ys_sem, yr_sem).wait_send()
            if k:
                z_copy(k, z_s, z_r, zs_sem, zr_sem).wait_send()

    my_live = counts[me] * BLOCK
    total = counts[0]
    for p in range(1, n_dp):
        total = total + counts[p]
    frame_total = (total * BLOCK).astype(jnp.float32)
    r_id = lax.broadcasted_iota(jnp.int32, (rows, slots), 0)
    s_id = lax.broadcasted_iota(jnp.int32, (rows, slots), 1)
    target = s_id
    end = 0
    for u in range(lengths.shape[1] - 1):
        end = end + lengths[0, u]
        target = target + jnp.where(s_id >= end, GAP, 0)
    place[...] = jnp.where((r_id == target) & (s_id < my_live), 1.0, 0.0).astype(jnp.bfloat16)
    put = place[...]
    live[...] = dot(put, jnp.ones((slots, chans), jnp.bfloat16))
    fg[...] = dot(put, frames[...]).astype(jnp.bfloat16)
    pre = dot(fg[...], proj[...])
    v = pre[:, :chans]
    g = jax.nn.sigmoid(pre[:, chans:])
    val[...] = v
    gate[...] = g
    pad = jnp.zeros((GAP, chans), jnp.float32)
    gpad[:GAP] = pad
    gpad[GAP + rows:] = pad
    cpad[:GAP] = pad
    cpad[GAP + rows:] = pad
    gpad[GAP:GAP + rows] = (v * g * live[...]).astype(jnp.bfloat16).astype(jnp.float32)

    half = rows // 2
    chunks = [(a, c) for a in range(0, rows, half) for c in range(0, chans, 128)]
    for a, c in chunks:
        acc = jnp.zeros((half, 128), jnp.float32)
        for k in range(tap_count):
            first = GAP + a + k - radius
            acc = acc + taps[k:k + 1, c:c + 128] * gpad[first:first + half, c:c + 128]
        conv[a:a + half, c:c + 128] = acc * live[a:a + half, c:c + 128]
    cv = conv[...]
    zero6 = jnp.zeros((6, chans), jnp.float32)
    st1[me] = jnp.concatenate(
        [jnp.sum(cv, axis=0, keepdims=True), jnp.sum(cv * cv, axis=0, keepdims=True), zero6], axis=0
    )
    pl.semaphore_wait(barrier, n_dp + n_mp - 2)
    exchange(st1, st1_s, st1_r)

    gg[...] = dot(put, grad_out[...]).astype(jnp.bfloat16)
    gh[...] = dot(gg[...], proj_out[...])

    exchange_wait(st1, st1_s, st1_r)
    sums = total_of(st1)
    mean = sums[0:1] / frame_total
    inv = lax.rsqrt(sums[1:2] / frame_total - mean * mean + 1e-05)
    normed = (conv[...] - mean) * inv
    scaled = normed * gain[...] + shift[...]
    sig = jax.nn.sigmoid(scaled)
    hidden = (scaled * sig * live[...]).astype(jnp.bfloat16)
    gscaled = gh[...] * live[...] * sig * (1.0 + scaled * (1.0 - sig))
    gs[...] = gscaled
    conv[...] = normed
    st2[me] = jnp.concatenate(
        [
            jnp.sum(gscaled, axis=0, keepdims=True),
            jnp.sum(gscaled * normed, axis=0, keepdims=True),
            zero6,
        ],
        axis=0,
    )
    exchange(st2, st2_s, st2_r)
    scatter_send(out_ring, gg, hidden)
    scatter_keep(out_ring, gg, hidden)

    exchange_wait(st2, st2_s, st2_r)
    sums = total_of(st2)
    o_shift[...] = sums[0:1]
    o_gain[...] = sums[1:2]
    cpad[GAP:GAP + rows] = (
        live[...] * (gain[...] * inv)
        * (gs[...] - sums[0:1] / frame_total - conv[...] * (sums[1:2] / frame_total))
    )
    out_steps = list(order)

    def half_grad(i):
        return jnp.concatenate(
            [gp[:, i * 128:i * 128 + 128], gp[:, chans + i * 128:chans + i * 128 + 128]], axis=1
        )

    for i, ring in enumerate(in_rings):
        c = i * 128
        for a in range(0, rows, half):
            acc = jnp.zeros((half, 128), jnp.float32)
            for k in range(tap_count):
                first = GAP + a + radius - k
                acc = acc + taps[k:k + 1, c:c + 128] * cpad[first:first + half, c:c + 128]
            acc = acc * live[a:a + half, c:c + 128]
            gt = gate[a:a + half, c:c + 128]
            gval = acc * gt
            gp[a:a + half, c:c + 128] = gval.astype(jnp.bfloat16)
            ggate = gval * val[a:a + half, c:c + 128] * (1.0 - gt)
            gp[a:a + half, chans + c:chans + c + 128] = ggate.astype(jnp.bfloat16)
            if out_steps:
                scatter_mid(out_ring, out_steps.pop(0))
        scatter_send(ring, fg, half_grad(i))
    for k in out_steps:
        scatter_mid(out_ring, k)

    def f_copy(k):
        return remote(f_s.at[k], f_r.at[k], fs_sem.at[k], fr_sem.at[k],
                      me, lax.rem(mp + k, n_mp))

    per = -(-tap_count // n_dp)

    def tap_sums(c):
        grad_c = cpad[GAP:GAP + rows, c:c + 128]
        for k in range(tap_count):
            first = GAP + k - radius
            d_s[k // per, k % per:k % per + 1, c:c + 128] = jnp.sum(
                grad_c * gpad[first:first + rows, c:c + 128], axis=0, keepdims=True
            )

    def d_copy(k):
        peer = lax.rem(me + k, n_dp)
        return remote(d_s.at[peer], d_r.at[k], ds_sem.at[k], dr_sem.at[k], peer, mp)

    d_s[...] = jnp.zeros(d_s.shape, jnp.float32)
    scatter_keep(in_rings[0], fg, half_grad(0))
    for k in order[:-1]:
        scatter_mid(in_rings[0], k)
    back = dot(place[...], gp[...], TN).astype(jnp.bfloat16)
    for k in list(range(1, n_mp)) + [0]:
        peer = lax.rem(mp + k, n_mp)
        part = proj[pl.ds(pl.multiple_of(peer * group, group), group), :]
        f_s[k] = dot(back, part, NT).astype(jnp.bfloat16)
        if k:
            f_copy(k).start()
    scatter_mid(in_rings[0], 0)
    for i in range(1, len(in_rings)):
        scatter_keep(in_rings[i], fg, half_grad(i))
    steps = [(ring, k) for ring in in_rings[1:] for k in order]
    for c in range(0, chans, 128):
        tap_sums(c)
        if steps:
            scatter_mid(*steps.pop(0))
    for k in range(1, n_dp):
        d_copy(k).start()
    for ring, k in steps:
        scatter_mid(ring, k)
    acc = d_s[me]
    for k in range(1, n_dp):
        d_copy(k).wait_recv()
        acc = acc + d_r[k]
    e_r[me] = acc
    exchange(e_r, es_sem, er_sem)

    o_out[...] = scatter_end(out_ring)
    facc = f_s[0].astype(jnp.float32)
    for k in range(1, n_mp):
        f_copy(k).wait_recv()
        facc = facc + f_r[k].astype(jnp.float32)
    o_frame[...] = facc.astype(jnp.bfloat16)
    for i, ring in enumerate(in_rings):
        both = scatter_end(ring)
        o_in[:, i * 128:i * 128 + 128] = both[:, :128]
        o_in[:, chans + i * 128:chans + i * 128 + 128] = both[:, 128:]
    exchange_wait(e_r, es_sem, er_sem)
    for p in range(n_dp):
        many = min(per, tap_count - p * per)
        if many > 0:
            o_depth[p * per:p * per + many] = e_r[p, :many]
    for ring in [out_ring] + in_rings:
        scatter_sent(ring)
    exchange_sent(st1, st1_s, st1_r)
    exchange_sent(st2, st2_s, st2_r)
    exchange_sent(e_r, es_sem, er_sem)
    for k in range(1, n_mp):
        f_copy(k).wait_send()
    for k in range(1, n_dp):
        d_copy(k).wait_send()


def hand_on(*refs):
    half = len(refs) // 2
    for src, dst in zip(refs[:half], refs[half:]):
        dst[...] = src[...]


def fused_shards(
    frames, proj_in, depthwise, bn_gain, bn_shift, proj_out, grad_out, counts, lengths
):
    n_dp, n_mp = lax.axis_size("dp"), lax.axis_size("mp")
    slots, width = frames.shape
    chans = proj_in.shape[2]
    tap_count = depthwise.shape[0]
    rows = slots + GAP * (lengths.shape[1] - 1)
    piece = width // n_dp
    group = width // n_mp
    nz = n_dp // 2
    per8 = -(-(-(-tap_count // n_dp)) // 8) * 8
    f32, bf16 = jnp.float32, jnp.bfloat16
    vm, dma = pltpu.VMEM, pltpu.SemaphoreType.DMA
    sem_pair = [dma((n_dp,)), dma((n_dp,))]

    def ring(wide):
        shape = (nz, piece, wide)
        return [vm(shape, bf16), vm(shape, bf16), vm(shape, f32), vm(shape, bf16),
                vm(shape, bf16)] + [dma((nz,))] * 4

    full = vm((rows, chans), f32)
    padded = vm((rows + 2 * GAP, chans), f32)
    in_vmem = pl.BlockSpec(memory_space=pltpu.VMEM)
    in_smem = pl.BlockSpec(memory_space=pltpu.SMEM)
    frame_grad, in_flat, out_grad, depth_grad, gain_grad, shift_grad = pl.pallas_call(
        functools.partial(fused, n_dp, n_mp),
        out_shape=[
            jax.ShapeDtypeStruct((slots, group), bf16),
            jax.ShapeDtypeStruct((piece, 2 * chans), f32),
            jax.ShapeDtypeStruct((piece, chans), f32),
            jax.ShapeDtypeStruct((tap_count, chans), f32),
            jax.ShapeDtypeStruct((1, chans), f32),
            jax.ShapeDtypeStruct((1, chans), f32),
        ],
        in_specs=[in_vmem] * 7 + [in_smem] * 2,
        out_specs=[in_vmem] * 6,
        scratch_shapes=[
            vm((rows, slots), bf16), full, vm((rows, width), bf16), vm((rows, width), bf16),
            padded, padded, full, full, full, full, full, vm((rows, 2 * chans), bf16),
            vm((n_dp, 8, chans), f32), *sem_pair, vm((n_dp, 8, chans), f32), *sem_pair,
            vm((n_mp, slots, group), bf16), vm((n_mp, slots, group), bf16),
            dma((n_mp,)), dma((n_mp,)),
            vm((n_dp, per8, chans), f32), vm((n_dp, per8, chans), f32), *sem_pair,
            vm((n_dp, per8, chans), f32), *sem_pair,
            *ring(chans), *(ref for _ in range(chans // 128) for ref in ring(256)),
        ],
        compiler_params=pltpu.CompilerParams(
            collective_id=0, has_side_effects=True, vmem_limit_bytes=48 * 1024 * 1024
        ),
    )(
        frames, proj_in.reshape(width, 2 * chans), depthwise, bn_gain[None], bn_shift[None],
        proj_out, grad_out, counts, lengths,
    )
    frame_grad, out_grad, depth_grad, gain_grad, shift_grad = pl.pallas_call(
        hand_on,
        out_shape=[
            jax.ShapeDtypeStruct(x.shape, x.dtype)
            for x in (frame_grad, out_grad, depth_grad, gain_grad, shift_grad)
        ],
        in_specs=[in_vmem] * 5,
        out_specs=[in_vmem] * 5,
    )(frame_grad, out_grad, depth_grad, gain_grad, shift_grad)
    return (
        frame_grad, in_flat.reshape(piece, 2, chans), out_grad, depth_grad,
        gain_grad.reshape(chans), shift_grad.reshape(chans),
    )


def pick(*args):
    n_dp = lax.axis_size("dp")
    frames, proj_in, taps = args[0], args[1], args[2]
    fits = (
        n_dp % 2 == 0 and n_dp <= 16 and frames.shape[1] % (128 * n_dp) == 0
        and proj_in.shape[2] % 128 == 0 and frames.shape[0] % 16 == 0
        and taps.shape[0] // 2 <= GAP
    )
    return (fused_shards if fits else shards)(*args)


def solution(mesh):
    placed = (
        P("dp", None),
        P(None, None, "mp"),
        P(None, "mp"),
        P("mp"),
        P("mp"),
        P(None, "mp"),
        P("dp", None),
        P(),
        P("dp", None),
    )
    return jax.shard_map(
        pick,
        mesh=mesh,
        in_specs=placed,
        out_specs=(
            P("dp", "mp"),
            P("dp", None, "mp"),
            P("dp", "mp"),
            P(None, "mp"),
            P("mp"),
            P("mp"),
        ),
        check_vma=False,
    )
```

```python
import functools

import jax
import jax.numpy as jnp
from jax import lax
from jax.experimental import pallas as pl
from jax.experimental.pallas import tpu as pltpu
from jax.sharding import PartitionSpec as P

BLOCK = 128


def time_shift(values, offset, fill_value):
    if offset > 0:
        pad_part = jnp.full((offset,) + values.shape[1:], fill_value, values.dtype)
        return jnp.concatenate([values[offset:], pad_part], axis=0)
    if offset < 0:
        pad_part = jnp.full((-offset,) + values.shape[1:], fill_value, values.dtype)
        return jnp.concatenate([pad_part, values[:offset]], axis=0)
    return values


def tap_term(glu_float, owner_id, live_col, offset):
    same_utt = (time_shift(owner_id, offset, -1) == owner_id).astype(jnp.float32)[
        :, None
    ] * live_col
    return time_shift(glu_float, offset, 0.0) * same_utt


def shards(frames, proj_in, depthwise, bn_gain, bn_shift, proj_out, grad_out, counts, lengths):
    frames_dev = frames.shape[0]
    model_width = frames.shape[1]
    channels = proj_in.shape[2]
    tap_count = depthwise.shape[0]
    radius = tap_count // 2
    rows_dev = model_width // lax.axis_size("dp")
    position = jnp.arange(frames_dev, dtype=jnp.int32)
    utt_ends = jnp.cumsum(lengths[0])
    owner_id = jnp.sum((position[:, None] >= utt_ends[None, :]).astype(jnp.int32), axis=1)
    my_count = counts[lax.axis_index("dp")]
    live_col = (position < my_count * BLOCK).astype(jnp.float32)[:, None]
    frame_total = (jnp.sum(counts) * BLOCK).astype(jnp.float32)
    proj_flat = proj_in.reshape(model_width, 2 * channels)
    pre_act = jnp.dot(frames, proj_flat, preferred_element_type=jnp.float32)
    value_half = pre_act[:, :channels]
    gate_sig = jax.nn.sigmoid(pre_act[:, channels:])
    glu_out = (value_half * gate_sig * live_col).astype(jnp.bfloat16)
    glu_float = lax.optimization_barrier(glu_out).astype(jnp.float32)
    conv_out = jnp.zeros((frames_dev, channels), jnp.float32)
    for tap_index in range(tap_count):
        conv_out = conv_out + depthwise[tap_index] * tap_term(
            glu_float, owner_id, live_col, tap_index - radius
        )
    sum_val, sum_sq = lax.psum(
        (jnp.sum(conv_out, axis=0), jnp.sum(conv_out * conv_out, axis=0)), "dp"
    )
    mean_val = sum_val / frame_total
    square_mean = sum_sq / frame_total
    inv_std = lax.rsqrt(square_mean - mean_val * mean_val + 1e-05)
    normed = (conv_out - mean_val) * inv_std
    scaled = normed * bn_gain + bn_shift
    sig_scaled = jax.nn.sigmoid(scaled)
    hidden = (scaled * sig_scaled * live_col).astype(jnp.bfloat16)
    grad_hidden = jnp.dot(grad_out, proj_out, preferred_element_type=jnp.float32) * live_col
    grad_scaled = grad_hidden * sig_scaled * (1.0 + scaled * (1.0 - sig_scaled))
    local_shift = jnp.sum(grad_scaled, axis=0)
    local_gain = jnp.sum(grad_scaled * normed, axis=0)
    shift_grad, gain_grad = lax.psum((local_shift, local_gain), "dp")
    grad_conv = (
        live_col
        * bn_gain
        * inv_std
        * (grad_scaled - shift_grad / frame_total - normed * gain_grad / frame_total)
    )
    depth_rows = []
    for tap_index in range(tap_count):
        depth_rows.append(
            jnp.sum(grad_conv * tap_term(glu_float, owner_id, live_col, tap_index - radius), axis=0)
        )
    depth_grad = lax.psum(jnp.stack(depth_rows), "dp")
    grad_glu = jnp.zeros((frames_dev, channels), jnp.float32)
    for tap_index in range(tap_count):
        offset = tap_index - radius
        back_same = (time_shift(owner_id, -offset, -1) == owner_id).astype(jnp.float32)[
            :, None
        ] * live_col
        grad_glu = grad_glu + depthwise[tap_index] * time_shift(grad_conv, -offset, 0.0) * back_same
    grad_value = grad_glu * gate_sig
    grad_gate = grad_glu * value_half * gate_sig * (1.0 - gate_sig)
    grad_flat = jnp.concatenate([grad_value, grad_gate], axis=1).astype(jnp.bfloat16)
    frame_term = lax.dot_general(
        grad_flat, proj_flat, (((1,), (1,)), ((), ())), preferred_element_type=jnp.float32
    )
    frame_grad = lax.psum_scatter(
        frame_term.astype(jnp.bfloat16), "mp", scatter_dimension=1, tiled=True
    )
    summed = lax.psum_scatter(
        jnp.concatenate(
            [
                lax.dot_general(
                    frames, grad_flat, (((0,), (0,)), ((), ())), preferred_element_type=jnp.float32
                ),
                lax.dot_general(
                    grad_out, hidden, (((0,), (0,)), ((), ())), preferred_element_type=jnp.float32
                ),
            ],
            axis=1,
        ),
        "dp",
        scatter_dimension=0,
        tiled=True,
    )
    in_flat = summed[:, : 2 * channels]
    out_grad = summed[:, 2 * channels :]
    in_grad = in_flat.reshape(rows_dev, 2, channels)
    return (frame_grad, in_grad, out_grad, depth_grad, gain_grad, shift_grad)


GAP = 16
NT = (((1,), (1,)), ((), ()))
TN = (((0,), (0,)), ((), ()))


def dot(a, b, dims=(((1,), (0,)), ((), ()))):
    return lax.dot_general(a, b, dims, preferred_element_type=jnp.float32)


def remote(src, dst, send_sem, recv_sem, dp, mp):
    return pltpu.make_async_remote_copy(
        src_ref=src,
        dst_ref=dst,
        send_sem=send_sem,
        recv_sem=recv_sem,
        device_id=(dp, mp),
        device_id_type=pl.DeviceIdType.MESH,
    )


def fused(
    n_dp, n_mp,
    frames, proj, taps, gain, shift, proj_out, grad_out, counts, lengths,
    o_frame, o_in, o_out, o_depth, o_gain, o_shift,
    place, live, fg, gg, gpad, cpad, val, gate, conv, gh, gs, gp,
    st1, st1_s, st1_r, st2, st2_s, st2_r,
    f_s, f_r, fs_sem, fr_sem,
    d_s, d_r, ds_sem, dr_sem, e_r, es_sem, er_sem,
    gsh, csh, *ring_refs,
):
    out_ring = ring_refs[:9]
    in_rings = [ring_refs[i:i + 9] for i in range(9, len(ring_refs), 9)]
    rows, chans = conv.shape
    slots = frames.shape[0]
    tap_count = taps.shape[0]
    radius = tap_count // 2
    me = lax.axis_index("dp")
    mp = lax.axis_index("mp")
    nz = n_dp // 2
    my_y = lax.rem(me, 2)
    my_z = me // 2
    piece = o_in.shape[0]
    group = o_frame.shape[1]

    barrier = pltpu.get_barrier_semaphore()
    for k in range(1, n_dp):
        pl.semaphore_signal(
            barrier, inc=1, device_id=(lax.rem(me + k, n_dp), mp),
            device_id_type=pl.DeviceIdType.MESH,
        )
    for k in range(1, n_mp):
        pl.semaphore_signal(
            barrier, inc=1, device_id=(me, lax.rem(mp + k, n_mp)),
            device_id_type=pl.DeviceIdType.MESH,
        )

    def exchange(buf, s_sem, r_sem):
        for k in range(1, n_dp):
            remote(buf.at[me], buf.at[me], s_sem.at[k - 1], r_sem.at[k - 1],
                   lax.rem(me + k, n_dp), mp).start()

    def exchange_wait(buf, s_sem, r_sem):
        for k in range(1, n_dp):
            who = lax.rem(me + n_dp - k, n_dp)
            c = remote(buf.at[who], buf.at[who], s_sem.at[k - 1], r_sem.at[k - 1], who, mp)
            c.wait_recv()

    def exchange_sent(buf, s_sem, r_sem):
        for k in range(1, n_dp):
            remote(buf.at[me], buf.at[me], s_sem.at[k - 1], r_sem.at[k - 1],
                   lax.rem(me + k, n_dp), mp).wait_send()

    def total_of(buf):
        acc = buf[0]
        for p in range(1, n_dp):
            acc = acc + buf[p]
        return acc

    order = list(range(1, nz)) + [0]

    def y_copy(k, s, r, s_sem, r_sem):
        return remote(s.at[k], r.at[k], s_sem.at[k], r_sem.at[k], my_z * 2 + 1 - my_y, mp)

    def z_copy(k, s, r, s_sem, r_sem):
        return remote(s.at[k], r.at[k], s_sem.at[k], r_sem.at[k],
                      lax.rem(my_z + k, nz) * 2 + my_y, mp)

    def scatter_send(ring, left, right):
        y_s, y_r, _, _, _, ys_sem, yr_sem, _, _ = ring
        for k in order:
            other = lax.rem(my_z + k, nz) * 2 + 1 - my_y
            cols = pl.ds(pl.multiple_of(other * piece, piece), piece)
            y_s[k] = dot(left[:, cols], right, TN).astype(jnp.bfloat16)
            y_copy(k, y_s, y_r, ys_sem, yr_sem).start()

    def scatter_keep(ring, left, right):
        for k in order:
            mine = lax.rem(my_z + k, nz) * 2 + my_y
            cols = pl.ds(pl.multiple_of(mine * piece, piece), piece)
            ring[2][k] = dot(left[:, cols], right, TN)

    def scatter_mid(ring, k):
        y_s, y_r, keep, z_s, z_r, ys_sem, yr_sem, zs_sem, zr_sem = ring
        y_copy(k, y_s, y_r, ys_sem, yr_sem).wait_recv()
        if k:
            z_s[k] = (keep[k] + y_r[k].astype(jnp.float32)).astype(jnp.bfloat16)
            z_copy(k, z_s, z_r, zs_sem, zr_sem).start()

    def scatter_end(ring):
        y_s, y_r, keep, z_s, z_r, ys_sem, yr_sem, zs_sem, zr_sem = ring
        acc = keep[0] + y_r[0].astype(jnp.float32)
        for k in range(1, nz):
            z_copy(k, z_s, z_r, zs_sem, zr_sem).wait_recv()
            acc = acc + z_r[k].astype(jnp.float32)
        return acc

    def scatter_sent(ring):
        y_s, y_r, keep, z_s, z_r, ys_sem, yr_sem, zs_sem, zr_sem = ring
        for k in range(nz):
            y_copy(k, y_s, y_r, ys_sem, yr_sem).wait_send()
            if k:
                z_copy(k, z_s, z_r, zs_sem, zr_sem).wait_send()

    my_live = counts[me] * BLOCK
    total = counts[0]
    for p in range(1, n_dp):
        total = total + counts[p]
    frame_total = (total * BLOCK).astype(jnp.float32)
    r_id = lax.broadcasted_iota(jnp.int32, (rows, slots), 0)
    s_id = lax.broadcasted_iota(jnp.int32, (rows, slots), 1)
    target = s_id
    end = 0
    for u in range(lengths.shape[1] - 1):
        end = end + lengths[0, u]
        target = target + jnp.where(s_id >= end, GAP, 0)
    place[...] = jnp.where((r_id == target) & (s_id < my_live), 1.0, 0.0).astype(jnp.bfloat16)
    put = place[...]
    live[...] = dot(put, jnp.ones((slots, chans), jnp.bfloat16))
    fg[...] = dot(put, frames[...]).astype(jnp.bfloat16)
    pre = dot(fg[...], proj[...])
    v = pre[:, :chans]
    g = jax.nn.sigmoid(pre[:, chans:])
    val[...] = v
    gate[...] = g
    pad = jnp.zeros((GAP, chans), jnp.float32)
    gpad[:GAP] = pad
    gpad[GAP + rows:] = pad
    cpad[:GAP] = pad
    cpad[GAP + rows:] = pad
    gpad[GAP:GAP + rows] = (v * g * live[...]).astype(jnp.bfloat16).astype(jnp.float32)

    span = rows + GAP + 8
    for j in range(8):
        gsh[j] = gpad[j:j + span]

    half = rows // 2
    chunks = [(a, c) for a in range(0, rows, half) for c in range(0, chans, 128)]
    for a, c in chunks:
        acc = jnp.zeros((half, 128), jnp.float32)
        for k in range(tap_count):
            first = GAP + a + k - radius
            acc = acc + taps[k:k + 1, c:c + 128] * gsh[first % 8, first - first % 8:first - first % 8 + half, c:c + 128]
        conv[a:a + half, c:c + 128] = acc * live[a:a + half, c:c + 128]
    cv = conv[...]
    zero6 = jnp.zeros((6, chans), jnp.float32)
    st1[me] = jnp.concatenate(
        [jnp.sum(cv, axis=0, keepdims=True), jnp.sum(cv * cv, axis=0, keepdims=True), zero6], axis=0
    )
    pl.semaphore_wait(barrier, n_dp + n_mp - 2)
    exchange(st1, st1_s, st1_r)

    gg[...] = dot(put, grad_out[...]).astype(jnp.bfloat16)
    gh[...] = dot(gg[...], proj_out[...])

    exchange_wait(st1, st1_s, st1_r)
    sums = total_of(st1)
    mean = sums[0:1] / frame_total
    inv = lax.rsqrt(sums[1:2] / frame_total - mean * mean + 1e-05)
    normed = (conv[...] - mean) * inv
    scaled = normed * gain[...] + shift[...]
    sig = jax.nn.sigmoid(scaled)
    hidden = (scaled * sig * live[...]).astype(jnp.bfloat16)
    gscaled = gh[...] * live[...] * sig * (1.0 + scaled * (1.0 - sig))
    gs[...] = gscaled
    conv[...] = normed
    st2[me] = jnp.concatenate(
        [
            jnp.sum(gscaled, axis=0, keepdims=True),
            jnp.sum(gscaled * normed, axis=0, keepdims=True),
            zero6,
        ],
        axis=0,
    )
    exchange(st2, st2_s, st2_r)
    scatter_send(out_ring, gg, hidden)
    scatter_keep(out_ring, gg, hidden)

    exchange_wait(st2, st2_s, st2_r)
    sums = total_of(st2)
    o_shift[...] = sums[0:1]
    o_gain[...] = sums[1:2]
    cpad[GAP:GAP + rows] = (
        live[...] * (gain[...] * inv)
        * (gs[...] - sums[0:1] / frame_total - conv[...] * (sums[1:2] / frame_total))
    )
    out_steps = list(order)

    def half_grad(i):
        return jnp.concatenate(
            [gp[:, i * 128:i * 128 + 128], gp[:, chans + i * 128:chans + i * 128 + 128]], axis=1
        )

    for i, ring in enumerate(in_rings):
        c = i * 128
        for j in range(8):
            csh[j, :, c:c + 128] = cpad[j:j + span, c:c + 128]
        for a in range(0, rows, half):
            acc = jnp.zeros((half, 128), jnp.float32)
            for k in range(tap_count):
                first = GAP + a + radius - k
                acc = acc + taps[k:k + 1, c:c + 128] * csh[first % 8, first - first % 8:first - first % 8 + half, c:c + 128]
            acc = acc * live[a:a + half, c:c + 128]
            gt = gate[a:a + half, c:c + 128]
            gval = acc * gt
            gp[a:a + half, c:c + 128] = gval.astype(jnp.bfloat16)
            ggate = gval * val[a:a + half, c:c + 128] * (1.0 - gt)
            gp[a:a + half, chans + c:chans + c + 128] = ggate.astype(jnp.bfloat16)
            if out_steps:
                scatter_mid(out_ring, out_steps.pop(0))
        scatter_send(ring, fg, half_grad(i))
    for k in out_steps:
        scatter_mid(out_ring, k)

    def f_copy(k):
        return remote(f_s.at[k], f_r.at[k], fs_sem.at[k], fr_sem.at[k],
                      me, lax.rem(mp + k, n_mp))

    per = -(-tap_count // n_dp)

    def tap_sums(c):
        grad_c = cpad[GAP:GAP + rows, c:c + 128]
        for k in range(tap_count):
            first = GAP + k - radius
            d_s[k // per, k % per:k % per + 1, c:c + 128] = jnp.sum(
                grad_c * gsh[first % 8, first - first % 8:first - first % 8 + rows, c:c + 128], axis=0, keepdims=True
            )

    def d_copy(k):
        peer = lax.rem(me + k, n_dp)
        return remote(d_s.at[peer], d_r.at[k], ds_sem.at[k], dr_sem.at[k], peer, mp)

    d_s[...] = jnp.zeros(d_s.shape, jnp.float32)
    scatter_keep(in_rings[0], fg, half_grad(0))
    for k in order[:-1]:
        scatter_mid(in_rings[0], k)
    back = dot(place[...], gp[...], TN).astype(jnp.bfloat16)
    for k in list(range(1, n_mp)) + [0]:
        peer = lax.rem(mp + k, n_mp)
        part = proj[pl.ds(pl.multiple_of(peer * group, group), group), :]
        f_s[k] = dot(back, part, NT).astype(jnp.bfloat16)
        if k:
            f_copy(k).start()
    scatter_mid(in_rings[0], 0)
    for i in range(1, len(in_rings)):
        scatter_keep(in_rings[i], fg, half_grad(i))
    steps = [(ring, k) for ring in in_rings[1:] for k in order]
    for c in range(0, chans, 128):
        tap_sums(c)
        if steps:
            scatter_mid(*steps.pop(0))
    for k in range(1, n_dp):
        d_copy(k).start()
    for ring, k in steps:
        scatter_mid(ring, k)
    acc = d_s[me]
    for k in range(1, n_dp):
        d_copy(k).wait_recv()
        acc = acc + d_r[k]
    e_r[me] = acc
    exchange(e_r, es_sem, er_sem)

    o_out[...] = scatter_end(out_ring)
    facc = f_s[0].astype(jnp.float32)
    for k in range(1, n_mp):
        f_copy(k).wait_recv()
        facc = facc + f_r[k].astype(jnp.float32)
    o_frame[...] = facc.astype(jnp.bfloat16)
    for i, ring in enumerate(in_rings):
        both = scatter_end(ring)
        o_in[:, i * 128:i * 128 + 128] = both[:, :128]
        o_in[:, chans + i * 128:chans + i * 128 + 128] = both[:, 128:]
    exchange_wait(e_r, es_sem, er_sem)
    for p in range(n_dp):
        many = min(per, tap_count - p * per)
        if many > 0:
            o_depth[p * per:p * per + many] = e_r[p, :many]
    for ring in [out_ring] + in_rings:
        scatter_sent(ring)
    exchange_sent(st1, st1_s, st1_r)
    exchange_sent(st2, st2_s, st2_r)
    exchange_sent(e_r, es_sem, er_sem)
    for k in range(1, n_mp):
        f_copy(k).wait_send()
    for k in range(1, n_dp):
        d_copy(k).wait_send()


def hand_on(*refs):
    half = len(refs) // 2
    copies = [
        pltpu.make_async_copy(refs[i], refs[half + i], refs[-1].at[i]) for i in range(half)
    ]
    for copy in copies:
        copy.start()
    for copy in copies:
        copy.wait()


def fused_shards(
    frames, proj_in, depthwise, bn_gain, bn_shift, proj_out, grad_out, counts, lengths
):
    n_dp, n_mp = lax.axis_size("dp"), lax.axis_size("mp")
    slots, width = frames.shape
    chans = proj_in.shape[2]
    tap_count = depthwise.shape[0]
    rows = slots + GAP * (lengths.shape[1] - 1)
    piece = width // n_dp
    group = width // n_mp
    nz = n_dp // 2
    per8 = -(-(-(-tap_count // n_dp)) // 8) * 8
    f32, bf16 = jnp.float32, jnp.bfloat16
    vm, dma = pltpu.VMEM, pltpu.SemaphoreType.DMA
    sem_pair = [dma((n_dp,)), dma((n_dp,))]

    def ring(wide):
        shape = (nz, piece, wide)
        return [vm(shape, bf16), vm(shape, bf16), vm(shape, f32), vm(shape, bf16),
                vm(shape, bf16)] + [dma((nz,))] * 4

    full = vm((rows, chans), f32)
    padded = vm((rows + 2 * GAP, chans), f32)
    in_vmem = pl.BlockSpec(memory_space=pltpu.VMEM)
    in_smem = pl.BlockSpec(memory_space=pltpu.SMEM)
    frame_grad, in_flat, out_grad, depth_grad, gain_grad, shift_grad = pl.pallas_call(
        functools.partial(fused, n_dp, n_mp),
        out_shape=[
            jax.ShapeDtypeStruct((slots, group), bf16),
            jax.ShapeDtypeStruct((piece, 2 * chans), f32),
            jax.ShapeDtypeStruct((piece, chans), f32),
            jax.ShapeDtypeStruct((tap_count, chans), f32),
            jax.ShapeDtypeStruct((1, chans), f32),
            jax.ShapeDtypeStruct((1, chans), f32),
        ],
        in_specs=[in_vmem] * 7 + [in_smem] * 2,
        out_specs=[in_vmem] * 6,
        scratch_shapes=[
            vm((rows, slots), bf16), full, vm((rows, width), bf16), vm((rows, width), bf16),
            padded, padded, full, full, full, full, full, vm((rows, 2 * chans), bf16),
            vm((n_dp, 8, chans), f32), *sem_pair, vm((n_dp, 8, chans), f32), *sem_pair,
            vm((n_mp, slots, group), bf16), vm((n_mp, slots, group), bf16),
            dma((n_mp,)), dma((n_mp,)),
            vm((n_dp, per8, chans), f32), vm((n_dp, per8, chans), f32), *sem_pair,
            vm((n_dp, per8, chans), f32), *sem_pair,
            vm((8, rows + GAP + 8, chans), f32), vm((8, rows + GAP + 8, chans), f32),
            *ring(chans), *(ref for _ in range(chans // 128) for ref in ring(256)),
        ],
        compiler_params=pltpu.CompilerParams(
            collective_id=0, has_side_effects=True, vmem_limit_bytes=48 * 1024 * 1024
        ),
    )(
        frames, proj_in.reshape(width, 2 * chans), depthwise, bn_gain[None], bn_shift[None],
        proj_out, grad_out, counts, lengths,
    )
    frame_grad, out_grad, depth_grad, gain_grad, shift_grad = pl.pallas_call(
        hand_on,
        out_shape=[
            jax.ShapeDtypeStruct(x.shape, x.dtype)
            for x in (frame_grad, out_grad, depth_grad, gain_grad, shift_grad)
        ],
        in_specs=[pl.BlockSpec(memory_space=pl.ANY)] * 5,
        out_specs=[pl.BlockSpec(memory_space=pl.ANY)] * 5,
        scratch_shapes=[dma((5,))],
    )(frame_grad, out_grad, depth_grad, gain_grad, shift_grad)
    return (
        frame_grad, in_flat.reshape(piece, 2, chans), out_grad, depth_grad,
        gain_grad.reshape(chans), shift_grad.reshape(chans),
    )


def pick(*args):
    n_dp = lax.axis_size("dp")
    frames, proj_in, taps = args[0], args[1], args[2]
    fits = (
        n_dp % 2 == 0 and n_dp <= 16 and frames.shape[1] % (128 * n_dp) == 0
        and proj_in.shape[2] % 128 == 0 and frames.shape[0] % 16 == 0
        and taps.shape[0] // 2 < GAP
    )
    return (fused_shards if fits else shards)(*args)


def solution(mesh):
    placed = (
        P("dp", None),
        P(None, None, "mp"),
        P(None, "mp"),
        P("mp"),
        P("mp"),
        P(None, "mp"),
        P("dp", None),
        P(),
        P("dp", None),
    )
    return jax.shard_map(
        pick,
        mesh=mesh,
        in_specs=placed,
        out_specs=(
            P("dp", "mp"),
            P("dp", None, "mp"),
            P("dp", "mp"),
            P(None, "mp"),
            P("mp"),
            P("mp"),
        ),
        check_vma=False,
    )
```

```python
import functools

import jax
import jax.numpy as jnp
from jax import lax
from jax.experimental import pallas as pl
from jax.experimental.pallas import tpu as pltpu
from jax.sharding import PartitionSpec as P

BLOCK = 128


def time_shift(values, offset, fill_value):
    if offset > 0:
        pad_part = jnp.full((offset,) + values.shape[1:], fill_value, values.dtype)
        return jnp.concatenate([values[offset:], pad_part], axis=0)
    if offset < 0:
        pad_part = jnp.full((-offset,) + values.shape[1:], fill_value, values.dtype)
        return jnp.concatenate([pad_part, values[:offset]], axis=0)
    return values


def tap_term(glu_float, owner_id, live_col, offset):
    same_utt = (time_shift(owner_id, offset, -1) == owner_id).astype(jnp.float32)[
        :, None
    ] * live_col
    return time_shift(glu_float, offset, 0.0) * same_utt


def shards(frames, proj_in, depthwise, bn_gain, bn_shift, proj_out, grad_out, counts, lengths):
    frames_dev = frames.shape[0]
    model_width = frames.shape[1]
    channels = proj_in.shape[2]
    tap_count = depthwise.shape[0]
    radius = tap_count // 2
    rows_dev = model_width // lax.axis_size("dp")
    position = jnp.arange(frames_dev, dtype=jnp.int32)
    utt_ends = jnp.cumsum(lengths[0])
    owner_id = jnp.sum((position[:, None] >= utt_ends[None, :]).astype(jnp.int32), axis=1)
    my_count = counts[lax.axis_index("dp")]
    live_col = (position < my_count * BLOCK).astype(jnp.float32)[:, None]
    frame_total = (jnp.sum(counts) * BLOCK).astype(jnp.float32)
    proj_flat = proj_in.reshape(model_width, 2 * channels)
    pre_act = jnp.dot(frames, proj_flat, preferred_element_type=jnp.float32)
    value_half = pre_act[:, :channels]
    gate_sig = jax.nn.sigmoid(pre_act[:, channels:])
    glu_out = (value_half * gate_sig * live_col).astype(jnp.bfloat16)
    glu_float = lax.optimization_barrier(glu_out).astype(jnp.float32)
    conv_out = jnp.zeros((frames_dev, channels), jnp.float32)
    for tap_index in range(tap_count):
        conv_out = conv_out + depthwise[tap_index] * tap_term(
            glu_float, owner_id, live_col, tap_index - radius
        )
    sum_val, sum_sq = lax.psum(
        (jnp.sum(conv_out, axis=0), jnp.sum(conv_out * conv_out, axis=0)), "dp"
    )
    mean_val = sum_val / frame_total
    square_mean = sum_sq / frame_total
    inv_std = lax.rsqrt(square_mean - mean_val * mean_val + 1e-05)
    normed = (conv_out - mean_val) * inv_std
    scaled = normed * bn_gain + bn_shift
    sig_scaled = jax.nn.sigmoid(scaled)
    hidden = (scaled * sig_scaled * live_col).astype(jnp.bfloat16)
    grad_hidden = jnp.dot(grad_out, proj_out, preferred_element_type=jnp.float32) * live_col
    grad_scaled = grad_hidden * sig_scaled * (1.0 + scaled * (1.0 - sig_scaled))
    local_shift = jnp.sum(grad_scaled, axis=0)
    local_gain = jnp.sum(grad_scaled * normed, axis=0)
    shift_grad, gain_grad = lax.psum((local_shift, local_gain), "dp")
    grad_conv = (
        live_col
        * bn_gain
        * inv_std
        * (grad_scaled - shift_grad / frame_total - normed * gain_grad / frame_total)
    )
    depth_rows = []
    for tap_index in range(tap_count):
        depth_rows.append(
            jnp.sum(grad_conv * tap_term(glu_float, owner_id, live_col, tap_index - radius), axis=0)
        )
    depth_grad = lax.psum(jnp.stack(depth_rows), "dp")
    grad_glu = jnp.zeros((frames_dev, channels), jnp.float32)
    for tap_index in range(tap_count):
        offset = tap_index - radius
        back_same = (time_shift(owner_id, -offset, -1) == owner_id).astype(jnp.float32)[
            :, None
        ] * live_col
        grad_glu = grad_glu + depthwise[tap_index] * time_shift(grad_conv, -offset, 0.0) * back_same
    grad_value = grad_glu * gate_sig
    grad_gate = grad_glu * value_half * gate_sig * (1.0 - gate_sig)
    grad_flat = jnp.concatenate([grad_value, grad_gate], axis=1).astype(jnp.bfloat16)
    frame_term = lax.dot_general(
        grad_flat, proj_flat, (((1,), (1,)), ((), ())), preferred_element_type=jnp.float32
    )
    frame_grad = lax.psum_scatter(
        frame_term.astype(jnp.bfloat16), "mp", scatter_dimension=1, tiled=True
    )
    summed = lax.psum_scatter(
        jnp.concatenate(
            [
                lax.dot_general(
                    frames, grad_flat, (((0,), (0,)), ((), ())), preferred_element_type=jnp.float32
                ),
                lax.dot_general(
                    grad_out, hidden, (((0,), (0,)), ((), ())), preferred_element_type=jnp.float32
                ),
            ],
            axis=1,
        ),
        "dp",
        scatter_dimension=0,
        tiled=True,
    )
    in_flat = summed[:, : 2 * channels]
    out_grad = summed[:, 2 * channels :]
    in_grad = in_flat.reshape(rows_dev, 2, channels)
    return (frame_grad, in_grad, out_grad, depth_grad, gain_grad, shift_grad)


GAP = 16
NT = (((1,), (1,)), ((), ()))
TN = (((0,), (0,)), ((), ()))


def dot(a, b, dims=(((1,), (0,)), ((), ()))):
    return lax.dot_general(a, b, dims, preferred_element_type=jnp.float32)


def remote(src, dst, send_sem, recv_sem, dp, mp):
    return pltpu.make_async_remote_copy(
        src_ref=src,
        dst_ref=dst,
        send_sem=send_sem,
        recv_sem=recv_sem,
        device_id=(dp, mp),
        device_id_type=pl.DeviceIdType.MESH,
    )


def fused(
    n_dp, n_mp,
    frames, proj, taps, gain, shift, proj_out, grad_out, counts, lengths,
    o_frame, o_in, o_out, o_depth, o_gain, o_shift,
    place, live, fg, gg, gpad, cpad, val, gate, conv, gh, gs, gp,
    st1, st1_s, st1_r, st2, st2_s, st2_r,
    f_s, f_r, fs_sem, fr_sem,
    d_s, d_r, ds_sem, dr_sem, e_r, es_sem, er_sem,
    gsh, csh, *ring_refs,
):
    out_ring = ring_refs[:9]
    in_rings = [ring_refs[i:i + 9] for i in range(9, len(ring_refs), 9)]
    rows, chans = conv.shape
    slots = frames.shape[0]
    tap_count = taps.shape[0]
    radius = tap_count // 2
    me = lax.axis_index("dp")
    mp = lax.axis_index("mp")
    nz = n_dp // 2
    my_y = lax.rem(me, 2)
    my_z = me // 2
    piece = o_in.shape[0]
    group = o_frame.shape[1]

    barrier = pltpu.get_barrier_semaphore()
    for k in range(1, n_dp):
        pl.semaphore_signal(
            barrier, inc=1, device_id=(lax.rem(me + k, n_dp), mp),
            device_id_type=pl.DeviceIdType.MESH,
        )
    for k in range(1, n_mp):
        pl.semaphore_signal(
            barrier, inc=1, device_id=(me, lax.rem(mp + k, n_mp)),
            device_id_type=pl.DeviceIdType.MESH,
        )

    def exchange(buf, s_sem, r_sem):
        for k in range(1, n_dp):
            remote(buf.at[me], buf.at[me], s_sem.at[k - 1], r_sem.at[k - 1],
                   lax.rem(me + k, n_dp), mp).start()

    def exchange_wait(buf, s_sem, r_sem):
        for k in range(1, n_dp):
            who = lax.rem(me + n_dp - k, n_dp)
            c = remote(buf.at[who], buf.at[who], s_sem.at[k - 1], r_sem.at[k - 1], who, mp)
            c.wait_recv()

    def exchange_sent(buf, s_sem, r_sem):
        for k in range(1, n_dp):
            remote(buf.at[me], buf.at[me], s_sem.at[k - 1], r_sem.at[k - 1],
                   lax.rem(me + k, n_dp), mp).wait_send()

    def total_of(buf):
        acc = buf[0]
        for p in range(1, n_dp):
            acc = acc + buf[p]
        return acc

    order = list(range(1, nz)) + [0]

    def y_copy(k, s, r, s_sem, r_sem):
        return remote(s.at[k], r.at[k], s_sem.at[k], r_sem.at[k], my_z * 2 + 1 - my_y, mp)

    def z_copy(k, s, r, s_sem, r_sem):
        return remote(s.at[k], r.at[k], s_sem.at[k], r_sem.at[k],
                      lax.rem(my_z + k, nz) * 2 + my_y, mp)

    def scatter_send(ring, left, right):
        y_s, y_r, _, _, _, ys_sem, yr_sem, _, _ = ring
        for k in order:
            other = lax.rem(my_z + k, nz) * 2 + 1 - my_y
            cols = pl.ds(pl.multiple_of(other * piece, piece), piece)
            y_s[k] = dot(left[:, cols], right, TN).astype(jnp.bfloat16)
            y_copy(k, y_s, y_r, ys_sem, yr_sem).start()

    def scatter_keep(ring, left, right):
        for k in order:
            mine = lax.rem(my_z + k, nz) * 2 + my_y
            cols = pl.ds(pl.multiple_of(mine * piece, piece), piece)
            ring[2][k] = dot(left[:, cols], right, TN)

    def scatter_mid(ring, k):
        y_s, y_r, keep, z_s, z_r, ys_sem, yr_sem, zs_sem, zr_sem = ring
        y_copy(k, y_s, y_r, ys_sem, yr_sem).wait_recv()
        if k:
            z_s[k] = (keep[k] + y_r[k].astype(jnp.float32)).astype(jnp.bfloat16)
            z_copy(k, z_s, z_r, zs_sem, zr_sem).start()

    def scatter_end(ring):
        y_s, y_r, keep, z_s, z_r, ys_sem, yr_sem, zs_sem, zr_sem = ring
        acc = keep[0] + y_r[0].astype(jnp.float32)
        for k in range(1, nz):
            z_copy(k, z_s, z_r, zs_sem, zr_sem).wait_recv()
            acc = acc + z_r[k].astype(jnp.float32)
        return acc

    def scatter_sent(ring):
        y_s, y_r, keep, z_s, z_r, ys_sem, yr_sem, zs_sem, zr_sem = ring
        for k in range(nz):
            y_copy(k, y_s, y_r, ys_sem, yr_sem).wait_send()
            if k:
                z_copy(k, z_s, z_r, zs_sem, zr_sem).wait_send()

    my_live = counts[me] * BLOCK
    total = counts[0]
    for p in range(1, n_dp):
        total = total + counts[p]
    frame_total = (total * BLOCK).astype(jnp.float32)
    r_id = lax.broadcasted_iota(jnp.int32, (rows, slots), 0)
    s_id = lax.broadcasted_iota(jnp.int32, (rows, slots), 1)
    target = s_id
    end = 0
    for u in range(lengths.shape[1] - 1):
        end = end + lengths[0, u]
        target = target + jnp.where(s_id >= end, GAP, 0)
    place[...] = jnp.where((r_id == target) & (s_id < my_live), 1.0, 0.0).astype(jnp.bfloat16)
    put = place[...]
    live[...] = dot(put, jnp.ones((slots, chans), jnp.bfloat16))
    fg[...] = dot(put, frames[...]).astype(jnp.bfloat16)
    pre = dot(fg[...], proj[...])
    v = pre[:, :chans]
    g = jax.nn.sigmoid(pre[:, chans:])
    val[...] = v
    gate[...] = g
    pad = jnp.zeros((GAP, chans), jnp.float32)
    gpad[:GAP] = pad
    gpad[GAP + rows:] = pad
    cpad[:GAP] = pad
    cpad[GAP + rows:] = pad
    gpad[GAP:GAP + rows] = (v * g * live[...]).astype(jnp.bfloat16).astype(jnp.float32)

    span = rows + GAP + 8
    for j in range(8):
        gsh[j] = gpad[j:j + span]

    half = rows // 2
    chunks = [(a, c) for a in range(0, rows, half) for c in range(0, chans, 128)]
    for a, c in chunks:
        acc = jnp.zeros((half, 128), jnp.float32)
        for k in range(tap_count):
            first = GAP + a + k - radius
            acc = acc + taps[k:k + 1, c:c + 128] * gsh[first % 8, first - first % 8:first - first % 8 + half, c:c + 128]
        conv[a:a + half, c:c + 128] = acc * live[a:a + half, c:c + 128]
    cv = conv[...]
    zero6 = jnp.zeros((6, chans), jnp.float32)
    st1[me] = jnp.concatenate(
        [jnp.sum(cv, axis=0, keepdims=True), jnp.sum(cv * cv, axis=0, keepdims=True), zero6], axis=0
    )
    pl.semaphore_wait(barrier, n_dp + n_mp - 2)
    exchange(st1, st1_s, st1_r)

    gg[...] = dot(put, grad_out[...]).astype(jnp.bfloat16)
    gh[...] = dot(gg[...], proj_out[...])

    exchange_wait(st1, st1_s, st1_r)
    sums = total_of(st1)
    mean = sums[0:1] / frame_total
    inv = lax.rsqrt(sums[1:2] / frame_total - mean * mean + 1e-05)
    normed = (conv[...] - mean) * inv
    scaled = normed * gain[...] + shift[...]
    sig = jax.nn.sigmoid(scaled)
    hidden = (scaled * sig * live[...]).astype(jnp.bfloat16)
    gscaled = gh[...] * live[...] * sig * (1.0 + scaled * (1.0 - sig))
    gs[...] = gscaled
    conv[...] = normed
    st2[me] = jnp.concatenate(
        [
            jnp.sum(gscaled, axis=0, keepdims=True),
            jnp.sum(gscaled * normed, axis=0, keepdims=True),
            zero6,
        ],
        axis=0,
    )
    exchange(st2, st2_s, st2_r)
    scatter_send(out_ring, gg, hidden)
    scatter_keep(out_ring, gg, hidden)

    exchange_wait(st2, st2_s, st2_r)
    sums = total_of(st2)
    o_shift[...] = sums[0:1]
    o_gain[...] = sums[1:2]
    cpad[GAP:GAP + rows] = (
        live[...] * (gain[...] * inv)
        * (gs[...] - sums[0:1] / frame_total - conv[...] * (sums[1:2] / frame_total))
    )
    out_steps = list(order)

    def half_grad(i):
        return jnp.concatenate(
            [gp[:, i * 128:i * 128 + 128], gp[:, chans + i * 128:chans + i * 128 + 128]], axis=1
        )

    for i, ring in enumerate(in_rings):
        c = i * 128
        for j in range(8):
            csh[j, :, c:c + 128] = cpad[j:j + span, c:c + 128]
        for a in range(0, rows, half):
            acc = jnp.zeros((half, 128), jnp.float32)
            for k in range(tap_count):
                first = GAP + a + radius - k
                acc = acc + taps[k:k + 1, c:c + 128] * csh[first % 8, first - first % 8:first - first % 8 + half, c:c + 128]
            acc = acc * live[a:a + half, c:c + 128]
            gt = gate[a:a + half, c:c + 128]
            gval = acc * gt
            gp[a:a + half, c:c + 128] = gval.astype(jnp.bfloat16)
            ggate = gval * val[a:a + half, c:c + 128] * (1.0 - gt)
            gp[a:a + half, chans + c:chans + c + 128] = ggate.astype(jnp.bfloat16)
            if out_steps:
                scatter_mid(out_ring, out_steps.pop(0))
        scatter_send(ring, fg, half_grad(i))
    for k in out_steps:
        scatter_mid(out_ring, k)

    def f_copy(k):
        return remote(f_s.at[k], f_r.at[k], fs_sem.at[k], fr_sem.at[k],
                      me, lax.rem(mp + k, n_mp))

    per = -(-tap_count // n_dp)

    def tap_sums(c):
        grad_c = cpad[GAP:GAP + rows, c:c + 128]
        for k in range(tap_count):
            first = GAP + k - radius
            d_s[k // per, k % per:k % per + 1, c:c + 128] = jnp.sum(
                grad_c * gsh[first % 8, first - first % 8:first - first % 8 + rows, c:c + 128], axis=0, keepdims=True
            )

    def d_copy(k):
        peer = lax.rem(me + k, n_dp)
        return remote(d_s.at[peer], d_r.at[k], ds_sem.at[k], dr_sem.at[k], peer, mp)

    d_s[...] = jnp.zeros(d_s.shape, jnp.float32)
    scatter_keep(in_rings[0], fg, half_grad(0))
    for k in order[:-1]:
        scatter_mid(in_rings[0], k)
    back = dot(place[...], gp[...], TN).astype(jnp.bfloat16)
    for k in list(range(1, n_mp)) + [0]:
        peer = lax.rem(mp + k, n_mp)
        part = proj[pl.ds(pl.multiple_of(peer * group, group), group), :]
        f_s[k] = dot(back, part, NT).astype(jnp.bfloat16)
        if k:
            f_copy(k).start()
    scatter_mid(in_rings[0], 0)
    for i in range(1, len(in_rings)):
        scatter_keep(in_rings[i], fg, half_grad(i))
    steps = [(ring, k) for ring in in_rings[1:] for k in order]
    for c in range(0, chans, 128):
        tap_sums(c)
        if steps:
            scatter_mid(*steps.pop(0))
    for k in range(1, n_dp):
        d_copy(k).start()
    for ring, k in steps:
        scatter_mid(ring, k)
    acc = d_s[me]
    for k in range(1, n_dp):
        d_copy(k).wait_recv()
        acc = acc + d_r[k]
    e_r[me] = acc
    exchange(e_r, es_sem, er_sem)

    o_out[...] = scatter_end(out_ring)
    facc = f_s[0].astype(jnp.float32)
    for k in range(1, n_mp):
        f_copy(k).wait_recv()
        facc = facc + f_r[k].astype(jnp.float32)
    o_frame[...] = facc.astype(jnp.bfloat16)
    for i, ring in enumerate(in_rings):
        both = scatter_end(ring)
        o_in[:, i * 128:i * 128 + 128] = both[:, :128]
        o_in[:, chans + i * 128:chans + i * 128 + 128] = both[:, 128:]
    exchange_wait(e_r, es_sem, er_sem)
    for p in range(n_dp):
        many = min(per, tap_count - p * per)
        if many > 0:
            o_depth[p * per:p * per + many] = e_r[p, :many]
    for ring in [out_ring] + in_rings:
        scatter_sent(ring)
    exchange_sent(st1, st1_s, st1_r)
    exchange_sent(st2, st2_s, st2_r)
    exchange_sent(e_r, es_sem, er_sem)
    for k in range(1, n_mp):
        f_copy(k).wait_send()
    for k in range(1, n_dp):
        d_copy(k).wait_send()


def fused_shards(
    frames, proj_in, depthwise, bn_gain, bn_shift, proj_out, grad_out, counts, lengths
):
    n_dp, n_mp = lax.axis_size("dp"), lax.axis_size("mp")
    slots, width = frames.shape
    chans = proj_in.shape[2]
    tap_count = depthwise.shape[0]
    rows = slots + GAP * (lengths.shape[1] - 1)
    piece = width // n_dp
    group = width // n_mp
    nz = n_dp // 2
    per8 = -(-(-(-tap_count // n_dp)) // 8) * 8
    f32, bf16 = jnp.float32, jnp.bfloat16
    vm, dma = pltpu.VMEM, pltpu.SemaphoreType.DMA
    sem_pair = [dma((n_dp,)), dma((n_dp,))]

    def ring(wide):
        shape = (nz, piece, wide)
        return [vm(shape, bf16), vm(shape, bf16), vm(shape, f32), vm(shape, bf16),
                vm(shape, bf16)] + [dma((nz,))] * 4

    full = vm((rows, chans), f32)
    padded = vm((rows + 2 * GAP, chans), f32)
    in_vmem = pl.BlockSpec(memory_space=pltpu.VMEM)
    in_smem = pl.BlockSpec(memory_space=pltpu.SMEM)
    frame_grad, in_flat, out_grad, depth_grad, gain_grad, shift_grad = pl.pallas_call(
        functools.partial(fused, n_dp, n_mp),
        out_shape=[
            jax.ShapeDtypeStruct((slots, group), bf16),
            jax.ShapeDtypeStruct((piece, 2 * chans), f32),
            jax.ShapeDtypeStruct((piece, chans), f32),
            jax.ShapeDtypeStruct((tap_count, chans), f32),
            jax.ShapeDtypeStruct((1, chans), f32),
            jax.ShapeDtypeStruct((1, chans), f32),
        ],
        in_specs=[in_vmem] * 7 + [in_smem] * 2,
        out_specs=[in_vmem] * 6,
        scratch_shapes=[
            vm((rows, slots), bf16), full, vm((rows, width), bf16), vm((rows, width), bf16),
            padded, padded, full, full, full, full, full, vm((rows, 2 * chans), bf16),
            vm((n_dp, 8, chans), f32), *sem_pair, vm((n_dp, 8, chans), f32), *sem_pair,
            vm((n_mp, slots, group), bf16), vm((n_mp, slots, group), bf16),
            dma((n_mp,)), dma((n_mp,)),
            vm((n_dp, per8, chans), f32), vm((n_dp, per8, chans), f32), *sem_pair,
            vm((n_dp, per8, chans), f32), *sem_pair,
            vm((8, rows + GAP + 8, chans), f32), vm((8, rows + GAP + 8, chans), f32),
            *ring(chans), *(ref for _ in range(chans // 128) for ref in ring(256)),
        ],
        compiler_params=pltpu.CompilerParams(
            collective_id=0, has_side_effects=True, vmem_limit_bytes=48 * 1024 * 1024
        ),
    )(
        frames, proj_in.reshape(width, 2 * chans), depthwise, bn_gain[None], bn_shift[None],
        proj_out, grad_out, counts, lengths,
    )
    return (
        frame_grad, in_flat.reshape(piece, 2, chans), out_grad, depth_grad,
        gain_grad.reshape(chans), shift_grad.reshape(chans),
    )


def pick(*args):
    n_dp = lax.axis_size("dp")
    frames, proj_in, taps = args[0], args[1], args[2]
    fits = (
        n_dp % 2 == 0 and n_dp <= 16 and frames.shape[1] % (128 * n_dp) == 0
        and proj_in.shape[2] % 128 == 0 and frames.shape[0] % 16 == 0
        and taps.shape[0] // 2 < GAP
    )
    return (fused_shards if fits else shards)(*args)


def solution(mesh):
    placed = (
        P("dp", None),
        P(None, None, "mp"),
        P(None, "mp"),
        P("mp"),
        P("mp"),
        P(None, "mp"),
        P("dp", None),
        P(),
        P("dp", None),
    )
    return jax.shard_map(
        pick,
        mesh=mesh,
        in_specs=placed,
        out_specs=(
            P("dp", "mp"),
            P("dp", None, "mp"),
            P("dp", "mp"),
            P(None, "mp"),
            P("mp"),
            P("mp"),
        ),
        check_vma=False,
    )
```
